512 devices in a mesh: grp: 32 (over y, x), head: 16 (over z, core).
Axes of the slice: x: 4, y: 8, z: 8, core: 2. Of those that a mesh axis runs over, the one named last changes fastest.
Arguments:
- q_nope: bfloat16 [4, 1024, 128, 128], P(None, 'grp', 'head'), may hold values from -6 to 6
- q_rope: bfloat16 [4, 1024, 128, 64], P(None, 'grp', 'head'), may hold values from -512 to 512
- w_absorb_k: bfloat16 [128, 128, 512], P('head'), may hold values from -0.5 to 0.5
- w_absorb_v: bfloat16 [128, 512, 128], P('head'), may hold values from -0.25 to 0.25
- latent_cache: bfloat16 [1024, 1024, 576], P(('grp', 'head')), may hold values from -4 to 4
- new_latent: bfloat16 [4, 1024, 576], P(None, ('grp', 'head')), may hold values from -6 to 6
- lengths: int32 [1024], replicated, may hold values from 128 to 1020, as said below
- moves: int32 [16, 1], P('head'), may hold values from 1 to 31
Outputs:
- attended: bfloat16 [4, 1024, 128, 128], P(None, 'grp', 'head')
The draws below stay inside these ranges and needn't reach their ends.
Inputs may be any that keep to these rules, and one draw needn't show every extreme that they name: lengths[r] counts the live rows of latent_cache[r]; its later rows up to 1024 are padding that no query reads.
All inputs are finite; a program needn't handle non-finite values.
Results may differ from the reference program's by a relative error of at most 0.0077.
Values may be sent and summed in bfloat16 or wider, within the bound.
No kernel may reach another device: no remote copies, remote signals or barrier semaphores. Data moves between devices by JAX's collectives and lax.ppermute only.
A program may use at most 64 MiB of HBM per device.

```python
import math
import jax
import jax.numpy as jnp
from jax import lax

HEADS = 128
HEAD_DIM = 128
ROPE = 64
LATENT = 512
BLOCK = 128
STEPS = 4
REQ_DEV = 2
KV = 576
CAP = 1024
MOVERS = 1
GROUPS = 32
COLUMNS = 16
REQUESTS = 1024


def first_keys(key):
    return jax.random.truncated_normal(jax.random.fold_in(key, 8), -4.0, 4.0, (REQUESTS, ROPE), jnp.float32)


def draw_latent_cache(key, part):
    shape = (REQUESTS, CAP, LATENT + ROPE)
    values = jax.random.truncated_normal(jax.random.fold_in(key, 7), -4.0, 4.0, shape, jnp.float32)
    values = values.at[:, 0, LATENT:].set(first_keys(key))
    return values.astype(jnp.bfloat16)


def draw_q_rope(key, part):
    shape = (STEPS, REQUESTS, HEADS, ROPE)
    values = jax.random.truncated_normal(jax.random.fold_in(key, 11), -4.0, 4.0, shape, jnp.float32)
    return values.astype(jnp.bfloat16)


def draw_lengths(key, part):
    spread_top = CAP - STEPS - BLOCK
    factor_one = jax.random.randint(jax.random.fold_in(key, 21), (REQUESTS,), 0, spread_top + 1)
    factor_two = jax.random.randint(jax.random.fold_in(key, 22), (REQUESTS,), 0, spread_top + 1)
    values = BLOCK + factor_one * factor_two // spread_top
    shuffled = jax.random.permutation(jax.random.fold_in(key, 23), REQUESTS)
    values = values.at[shuffled[0]].set(CAP - STEPS).at[shuffled[1]].set(BLOCK)
    return values.astype(jnp.int32)


def draw_moves(key, part):
    values = jax.random.randint(jax.random.fold_in(key, 31), (COLUMNS, MOVERS), 1, GROUPS)
    forced_at = jax.random.randint(jax.random.fold_in(key, 32), (), 0, COLUMNS * MOVERS)
    flattened = values.reshape(-1).at[forced_at].set(GROUPS - 1)
    return flattened.reshape(COLUMNS, MOVERS).astype(jnp.int32)


def block_scale(stream_key, dims, pieces, low, high):
    def one(dim, shards_of):
        draws = jax.random.uniform(jax.random.fold_in(jax.random.fold_in(stream_key, 6), dim), (shards_of,), jnp.float32, low / len(pieces), high / len(pieces))
        return jnp.repeat(jnp.exp(draws), dims[dim] // shards_of).reshape((-1,) + (1,) * (len(dims) - dim - 1))

    factor_of = one(*pieces[0])
    for cut in pieces[1:]:
        factor_of = factor_of * one(*cut)
    return factor_of


def normal_values(rng, dims, width, most, cuts=(), kind=jnp.bfloat16):
    result = width * jax.random.normal(rng, dims, jnp.float32)
    if cuts:
        result = result * block_scale(rng, dims, cuts, -0.22, 0.18)
    return jnp.clip(result, -most, most).astype(kind)


def setup_inputs(seed: int = 0) -> dict:
    splits = jax.random.split(jax.random.key(seed), 9)
    return {
        "q_nope": normal_values(splits[0], (STEPS, REQUESTS, HEADS, HEAD_DIM), 1.0, 6.0, ((1, 32), (2, 16))),
        "q_rope": draw_q_rope(jax.random.fold_in(splits[8], 71), 0),
        "w_absorb_k": normal_values(splits[2], (HEADS, HEAD_DIM, LATENT), HEAD_DIM ** -0.5, 0.5, ((0, 16),)),
        "w_absorb_v": normal_values(splits[3], (HEADS, LATENT, HEAD_DIM), LATENT ** -0.5, 0.25, ((0, 16),)),
        "latent_cache": draw_latent_cache(jax.random.fold_in(splits[8], 71), 0),
        "new_latent": normal_values(splits[5], (STEPS, REQUESTS, KV), 1.0, 6.0, ((1, 512),)),
        "lengths": draw_lengths(jax.random.fold_in(splits[8], 71), 0),
        "moves": draw_moves(jax.random.fold_in(splits[8], 71), 0),
    }


yarn_gain = (0.1 * math.log(40.0) + 1.0) ** 2

def home_slots(moves):
    group_ids = jnp.arange(GROUPS, dtype=jnp.int32)[:, None, None]
    column_ids = jnp.arange(COLUMNS, dtype=jnp.int32)[None, :, None]
    place_ids = jnp.arange(REQ_DEV, dtype=jnp.int32)[None, None, :]
    offsets = jnp.concatenate([moves.astype(jnp.int32), jnp.zeros((COLUMNS, REQ_DEV - MOVERS), jnp.int32)], axis=1)[None, :, :]
    source = jnp.mod(group_ids - offsets, GROUPS)
    return ((source * COLUMNS + column_ids) * REQ_DEV + place_ids).reshape(-1).astype(jnp.int32)

def attend_one(query_row, stored, live_count, recent, live_steps, score_scale):
    query_wide = query_row.astype(jnp.float32)
    scores = jnp.einsum('hc,tc->ht', query_wide, stored.astype(jnp.float32)) * score_scale
    positions = jnp.arange(stored.shape[0], dtype=jnp.int32)
    scores = jnp.where(positions[None, :] < live_count, scores, -jnp.inf)
    extra_scores = jnp.einsum('hc,jc->hj', query_wide, recent.astype(jnp.float32)) * score_scale
    extra_scores = jnp.where(live_steps[None, :], extra_scores, -jnp.inf)
    peak = jnp.maximum(lax.optimization_barrier(jnp.max(scores, axis=1)), lax.optimization_barrier(jnp.max(extra_scores, axis=1)))[:, None]
    spread = jnp.exp(scores - peak)
    spread_new = jnp.exp(extra_scores - peak)
    softmax_sum = lax.optimization_barrier(jnp.sum(spread, axis=1, keepdims=True)) + lax.optimization_barrier(jnp.sum(spread_new, axis=1, keepdims=True))
    weights = lax.optimization_barrier((spread / softmax_sum).astype(jnp.bfloat16)).astype(jnp.float32)
    weights_new = lax.optimization_barrier((spread_new / softmax_sum).astype(jnp.bfloat16)).astype(jnp.float32)
    mixed_rows = jnp.einsum('ht,tl->hl', weights, stored[:, :LATENT].astype(jnp.float32))
    mixed_rows = mixed_rows + jnp.einsum('hj,jl->hl', weights_new, recent[:, :LATENT].astype(jnp.float32))
    return mixed_rows.astype(jnp.bfloat16)

def reference(q_nope, q_rope, w_absorb_k, w_absorb_v, latent_cache, new_latent, lengths, moves):
    score_scale = yarn_gain / math.sqrt(HEAD_DIM + ROPE)
    own_rows = jnp.arange(REQUESTS, dtype=jnp.int32)
    moved_rows = home_slots(moves)
    batch_rows = COLUMNS * REQ_DEV
    step_ids = jnp.arange(STEPS, dtype=jnp.int32)
    results = []
    for moment in range(STEPS):
        home_rows = moved_rows if moment >= 2 else own_rows
        root = jnp.where(step_ids[None, :] < 2, home_rows[:, None], own_rows[:, None]).astype(jnp.int32)
        live_steps = step_ids <= moment
        q_latent = jnp.einsum('rhd,hdl->rhl', q_nope[moment].astype(jnp.float32), w_absorb_k.astype(jnp.float32)).astype(jnp.bfloat16)
        queries = jnp.concatenate([q_latent, q_rope[moment]], axis=2)

        def one_block(element):
            block_queries, block_home, block_root = element

            def one_request(query_row, source, chosen_rows):
                stored = lax.dynamic_index_in_dim(latent_cache, source, 0, keepdims=False)
                recent = new_latent[step_ids, chosen_rows]
                live_count = lengths[source]
                return attend_one(query_row, stored, live_count, recent, live_steps, score_scale)
            return jax.vmap(one_request)(block_queries, block_home, block_root)
        mixed_rows = lax.map(one_block, (queries.reshape(-1, batch_rows, HEADS, queries.shape[2]), home_rows.reshape(-1, batch_rows), root.reshape(-1, batch_rows, STEPS)))
        mixed_rows = mixed_rows.reshape(REQUESTS, HEADS, LATENT)
        results.append(jnp.einsum('rhl,hld->rhd', mixed_rows.astype(jnp.float32), w_absorb_v.astype(jnp.float32)).astype(jnp.bfloat16))
    return jnp.stack(results)
```

```python
import functools
import math

import jax
import jax.numpy as jnp
from jax import lax
from jax.experimental import pallas as pl
from jax.experimental.pallas import tpu as pltpu
from jax.sharding import PartitionSpec as P

HEAD_DIM = 128
ROPE = 64
LATENT = 512
LANES = 128
CHUNKS = LATENT // LANES
UNIT = 16
HIDDEN = -1e30

yarn_gain = (0.1 * math.log(40.0) + 1.0) ** 2
score_scale = yarn_gain / math.sqrt(HEAD_DIM + ROPE)


def split_places(rows, columns):
    wide = rows.astype(jnp.float32).reshape(columns, 2, 8, rows.shape[-1])
    return wide[:, 0], wide[:, 1]


def absorb_kernel(q_ref, r_ref, w_ref, held_ref, moved_ref):
    columns = held_ref.shape[0]
    heads = w_ref.shape[0]
    weights = w_ref[...].reshape(heads * HEAD_DIM, LATENT)
    lane_head = lax.broadcasted_iota(jnp.int32, (columns, UNIT, HEAD_DIM), 1) % heads
    nope = [split_places(q_ref[step], columns) for step in range(4)]
    rope = [split_places(r_ref[step], columns) for step in range(4)]

    def unit_of(parts, first, place):
        return jnp.concatenate([parts[first][place], parts[first + 1][place]], axis=1)

    units = [(2, 0), (0, 0), (0, 1), (2, 1)]
    for number, (first, place) in enumerate(units):
        rows = unit_of(nope, first, place)
        spread = jnp.concatenate(
            [
                jnp.where(lane_head == head, rows, 0.0)
                .astype(jnp.bfloat16)
                .reshape(columns * UNIT, HEAD_DIM)
                for head in range(heads)
            ],
            axis=1,
        )
        latent = jnp.dot(spread, weights, preferred_element_type=jnp.float32)
        latent = latent.astype(jnp.bfloat16).reshape(columns, UNIT, LATENT)
        for chunk in range(CHUNKS):
            piece = latent[:, :, chunk * LANES : (chunk + 1) * LANES]
            if number == 0:
                moved_ref[:, pl.ds(chunk * UNIT, UNIT), :] = piece
            else:
                at = ((number - 1) * CHUNKS + chunk) * UNIT
                held_ref[:, pl.ds(at, UNIT), :] = piece
    blank = jnp.zeros((columns, UNIT, ROPE), jnp.float32)
    at = 3 * CHUNKS * UNIT
    pair = jnp.concatenate([unit_of(rope, 0, 0), unit_of(rope, 0, 1)], axis=2)
    held_ref[:, pl.ds(at, UNIT), :] = pair.astype(jnp.bfloat16)
    single = jnp.concatenate([unit_of(rope, 2, 1), blank], axis=2)
    held_ref[:, pl.ds(at + UNIT, UNIT), :] = single.astype(jnp.bfloat16)
    single = jnp.concatenate([unit_of(rope, 2, 0), blank], axis=2)
    moved_ref[:, pl.ds(CHUNKS * UNIT, UNIT), :] = single.astype(jnp.bfloat16)


def absorb(q_nope, q_rope, w_absorb_k, columns):
    return pl.pallas_call(
        absorb_kernel,
        out_shape=(
            jax.ShapeDtypeStruct((columns, 14 * UNIT, LANES), jnp.bfloat16),
            jax.ShapeDtypeStruct((columns, 5 * UNIT, LANES), jnp.bfloat16),
        ),
        compiler_params=pltpu.CompilerParams(vmem_limit_bytes=32 * 1024 * 1024),
        cost_estimate=pl.CostEstimate(
            flops=1024 * 1024 * 512 * 2, bytes_accessed=3 * 1024 * 1024, transcendentals=0
        ),
        name="absorb",
    )(q_nope, q_rope, w_absorb_k)


def attend_unit(query, keys_ref, count, first_step):
    rows = query.shape[0]
    keys = keys_ref[...]
    capacity = keys.shape[0]
    scores = lax.dot_general(
        query, keys, (((1,), (1,)), ((), ())), preferred_element_type=jnp.float32
    )
    position = lax.broadcasted_iota(jnp.int32, (rows, capacity), 1)
    step = first_step + lax.broadcasted_iota(jnp.int32, (rows, 1), 0) % UNIT // 8
    scores = jnp.where(position < count + step + 1, scores * score_scale, HIDDEN)
    peak = jnp.max(scores, axis=1, keepdims=True)
    spread = jnp.exp(scores - peak)
    total = jnp.sum(spread, axis=1, keepdims=True)
    mixed = jnp.dot(
        spread.astype(jnp.bfloat16), keys[:, :LATENT], preferred_element_type=jnp.float32
    )
    return (mixed / total).astype(jnp.bfloat16)


def place_recent(keys_ref, recent, count):
    capacity = keys_ref.shape[0]
    start = jnp.minimum(count // UNIT * UNIT, capacity - 2 * UNIT)
    start = pl.multiple_of(start, UNIT)
    window = keys_ref[pl.ds(start, 2 * UNIT), :].astype(jnp.float32)
    row = start + lax.broadcasted_iota(jnp.int32, window.shape, 0)
    for step in range(recent.shape[0]):
        window = jnp.where(row == count + step, recent[step : step + 1], window)
    keys_ref[pl.ds(start, 2 * UNIT), :] = window.astype(jnp.bfloat16)


def unit_query(got_ref, at, rope):
    columns = got_ref.shape[0]
    parts = [
        got_ref[:, pl.ds(at + chunk * UNIT, UNIT), :].reshape(columns * UNIT, LANES)
        for chunk in range(CHUNKS)
    ]
    return jnp.concatenate(parts + [rope], axis=1)


def put_unit(out_ref, at, mixed):
    columns = out_ref.shape[0]
    mixed = mixed.reshape(columns, UNIT, LATENT)
    for chunk in range(CHUNKS):
        out_ref[:, pl.ds(at + chunk * UNIT, UNIT), :] = mixed[
            :, :, chunk * LANES : (chunk + 1) * LANES
        ]


def held_kernel(counts_ref, got_ref, cache_ref, recent_ref, out_ref, keys_ref, sems):
    columns = got_ref.shape[0]
    copies = [
        pltpu.make_async_copy(cache_ref.at[place], keys_ref.at[place], sems.at[place])
        for place in range(2)
    ]
    for copy in copies:
        copy.start()
    recent = recent_ref[...].astype(jnp.float32)
    ropes = got_ref[:, pl.ds(3 * CHUNKS * UNIT, UNIT), :].reshape(columns * UNIT, LANES)
    late = got_ref[:, pl.ds(3 * CHUNKS * UNIT + UNIT, UNIT), :].reshape(columns * UNIT, LANES)
    wide = [ropes[:, :ROPE], ropes[:, ROPE:], late[:, :ROPE]]
    for place in range(2):
        copies[place].wait()
        keys = keys_ref.at[place]
        count = counts_ref[place]
        place_recent(keys, recent[:, place], count)
        for unit, first_step in ([(0, 0)], [(1, 0), (2, 2)])[place]:
            at = unit * CHUNKS * UNIT
            mixed = attend_unit(unit_query(got_ref, at, wide[unit]), keys, count, first_step)
            put_unit(out_ref, at, mixed)


def moved_kernel(counts_ref, got_ref, cache_ref, recent_ref, out_ref, keys_ref, sem):
    columns = got_ref.shape[0]
    copy = pltpu.make_async_copy(cache_ref.at[0], keys_ref, sem)
    copy.start()
    recent = recent_ref[...].astype(jnp.float32)
    rope = got_ref[:, pl.ds(CHUNKS * UNIT, UNIT), :].reshape(columns * UNIT, LANES)[:, :ROPE]
    copy.wait()
    count = counts_ref[0]
    place_recent(keys_ref, recent, count)
    put_unit(out_ref, 0, attend_unit(unit_query(got_ref, 0, rope), keys_ref, count, 2))


def attend(kernel, got, cache, recent, counts, units, keys_shape, sem_shape, name):
    columns = got.shape[0]
    vmem = pl.BlockSpec(memory_space=pltpu.VMEM)
    return pl.pallas_call(
        kernel,
        out_shape=jax.ShapeDtypeStruct((columns, units * CHUNKS * UNIT, LANES), jnp.bfloat16),
        in_specs=[
            pl.BlockSpec(memory_space=pltpu.SMEM),
            vmem,
            pl.BlockSpec(memory_space=pl.ANY),
            vmem,
        ],
        out_specs=vmem,
        scratch_shapes=[
            pltpu.VMEM(keys_shape, jnp.bfloat16),
            pltpu.SemaphoreType.DMA(sem_shape),
        ],
        compiler_params=pltpu.CompilerParams(vmem_limit_bytes=32 * 1024 * 1024),
        cost_estimate=pl.CostEstimate(
            flops=units * 256 * 1024 * 1152 * 2,
            bytes_accessed=units * 2 * 1024 * 1024,
            transcendentals=units * 256 * 1024,
        ),
        name=name,
    )(counts, got, cache, recent)


def project_unit(got_ref, at, w_ref):
    columns = got_ref.shape[0]
    heads = w_ref.shape[0]
    parts = [
        got_ref[:, pl.ds(at + chunk * UNIT, UNIT), :].reshape(columns * UNIT, LANES)
        for chunk in range(CHUNKS)
    ]
    latent = jnp.concatenate(parts, axis=1)
    row_head = lax.broadcasted_iota(jnp.int32, (columns * UNIT, HEAD_DIM), 0) % heads
    result = jnp.zeros((columns * UNIT, HEAD_DIM), jnp.float32)
    for head in range(0, heads, 2):
        pair = jnp.concatenate([w_ref[head], w_ref[head + 1]], axis=1)
        product = jnp.dot(latent, pair, preferred_element_type=jnp.float32)
        result = jnp.where(row_head == head, product[:, :HEAD_DIM], result)
        result = jnp.where(row_head == head + 1, product[:, HEAD_DIM:], result)
    result = result.reshape(columns, 2, 8, HEAD_DIM)
    return result[:, 0], result[:, 1]


def project_kernel(held_ref, moved_ref, w_ref, out_ref):
    columns = held_ref.shape[0]
    span = CHUNKS * UNIT
    for first, (near_ref, near_at), (far_ref, far_at) in (
        (0, (held_ref, 0), (held_ref, span)),
        (2, (moved_ref, 0), (held_ref, 2 * span)),
    ):
        near = project_unit(near_ref, near_at, w_ref)
        far = project_unit(far_ref, far_at, w_ref)
        for step in range(2):
            rows = jnp.concatenate([near[step], far[step]], axis=1)
            out_ref[first + step] = rows.astype(jnp.bfloat16).reshape(
                columns * UNIT, HEAD_DIM
            )


def project(held, moved, w_absorb_v):
    columns = held.shape[0]
    return pl.pallas_call(
        project_kernel,
        out_shape=jax.ShapeDtypeStruct((4, columns * UNIT, HEAD_DIM), jnp.bfloat16),
        compiler_params=pltpu.CompilerParams(vmem_limit_bytes=32 * 1024 * 1024),
        cost_estimate=pl.CostEstimate(
            flops=1024 * 1024 * 512 * 2, bytes_accessed=3 * 1024 * 1024, transcendentals=0
        ),
        name="project",
    )(held, moved, w_absorb_v)


def shifted(value, shift, sign):
    count = lax.axis_size("grp")

    def along(steps):
        pairs = [(source, (source + steps) % count) for source in range(count)]
        return lambda given: lax.ppermute(given, "grp", pairs)

    branches = [along(sign * steps) for steps in range(1, count)]
    return lax.switch(shift - 1, branches, value)


def exchanged(value):
    return lax.all_to_all(value, "head", split_axis=0, concat_axis=0, tiled=True)


def body(q_nope, q_rope, w_absorb_k, w_absorb_v, latent_cache, new_latent, lengths, moves):
    steps, slots, heads, _ = q_nope.shape
    holders, capacity, entries = latent_cache.shape
    columns = lax.axis_size("head")
    shift = moves[0, 0]
    first_slot = (lax.axis_index("grp") * columns + lax.axis_index("head")) * holders
    counts = lax.dynamic_slice_in_dim(lengths, first_slot, holders)

    held_out, moved_out = absorb(
        q_nope.reshape(steps, slots * heads, HEAD_DIM),
        q_rope.reshape(steps, slots * heads, ROPE),
        w_absorb_k,
        columns,
    )
    moved_in = exchanged(moved_out)
    held_in = exchanged(held_out)
    fresh = shifted(new_latent[2:, 0], shift, -1)
    moved_in = shifted(moved_in, shift, -1)
    moved_recent = jnp.concatenate([new_latent[:2, 0], fresh], axis=0)
    moved_mixed = attend(
        moved_kernel, moved_in, latent_cache, moved_recent, counts, 1, (capacity, entries), (), "moved"
    )
    held_mixed = attend(
        held_kernel,
        held_in,
        latent_cache,
        new_latent,
        counts,
        3,
        (holders, capacity, entries),
        (2,),
        "held",
    )
    held_back = exchanged(held_mixed)
    moved_back = exchanged(shifted(moved_mixed, shift, 1))
    out = project(held_back, moved_back, w_absorb_v)
    return out.reshape(steps, slots, heads, HEAD_DIM)


def solution(mesh):
    placed = (
        P(None, "grp", "head", None),
        P(None, "grp", "head", None),
        P("head", None, None),
        P("head", None, None),
        P(("grp", "head"), None, None),
        P(None, ("grp", "head"), None),
        P(),
        P("head", None),
    )
    return jax.shard_map(
        body, mesh=mesh, in_specs=placed, out_specs=P(None, "grp", "head", None), check_vma=False
    )
```

```python
import functools
import math

import jax
import jax.numpy as jnp
from jax import lax
from jax.experimental import pallas as pl
from jax.experimental.pallas import tpu as pltpu
from jax.sharding import PartitionSpec as P

HEAD_DIM = 128
ROPE = 64
LATENT = 512
LANES = 128
CHUNKS = LATENT // LANES
UNIT = 16
HIDDEN = -1e30

yarn_gain = (0.1 * math.log(40.0) + 1.0) ** 2
score_scale = yarn_gain / math.sqrt(HEAD_DIM + ROPE)


def split_places(rows, columns):
    wide = rows.astype(jnp.float32).reshape(columns, 2, 8, rows.shape[-1])
    return wide[:, 0], wide[:, 1]


def spread_heads(rows, heads):
    columns = rows.shape[0]
    lane_head = lax.broadcasted_iota(jnp.int32, rows.shape, 1) % heads
    pieces = [
        jnp.where(lane_head == head, rows, 0.0)
        .astype(jnp.bfloat16)
        .reshape(columns * UNIT, HEAD_DIM)
        for head in range(heads)
    ]
    return jnp.concatenate(pieces, axis=1)


def absorb_kernel(steps, units, q_hbm, r_hbm, w_hbm, out_ref, q_ref, r_ref, w_ref, sems):
    columns = out_ref.shape[0]
    heads = w_ref.shape[0]
    first = steps[0]
    copies = [
        pltpu.make_async_copy(q_hbm.at[pl.ds(first, len(steps))], q_ref, sems.at[0]),
        pltpu.make_async_copy(r_hbm.at[pl.ds(first, len(steps))], r_ref, sems.at[1]),
        pltpu.make_async_copy(w_hbm, w_ref, sems.at[2]),
    ]
    for copy in copies:
        copy.start()
    copies[0].wait()
    nope = {step: split_places(q_ref[step - first], columns) for step in steps}
    copies[1].wait()
    rope = {step: split_places(r_ref[step - first], columns) for step in steps}

    def unit_of(parts, begin, place):
        return jnp.concatenate([parts[begin][place], parts[begin + 1][place]], axis=1)

    blank = jnp.zeros((columns, UNIT, ROPE), jnp.float32)
    for number in range(0, len(units), 2):
        pair = [unit_of(rope, *unit) for unit in units[number : number + 2]] + [blank]
        at = (len(units) * CHUNKS + number // 2) * UNIT
        both = jnp.concatenate(pair[:2], axis=2).astype(jnp.bfloat16)
        out_ref[:, pl.ds(at, UNIT), :] = both
    copies[2].wait()
    weights = w_ref[...].reshape(heads * HEAD_DIM, LATENT)
    for number, unit in enumerate(units):
        spread = spread_heads(unit_of(nope, *unit), heads)
        latent = jnp.dot(spread, weights, preferred_element_type=jnp.float32)
        put_unit(out_ref, number * CHUNKS * UNIT, latent.astype(jnp.bfloat16))


def absorb(q_nope, q_rope, w_absorb_k, columns, steps, units, name):
    high = len(units) * CHUNKS + (len(units) + 1) // 2
    hbm = pl.BlockSpec(memory_space=pltpu.HBM)
    slots = q_nope.shape[1]
    return pl.pallas_call(
        functools.partial(absorb_kernel, steps, units),
        out_shape=pltpu.HBM((columns, high * UNIT, LANES), jnp.bfloat16),
        in_specs=[hbm] * 3,
        scratch_shapes=[
            pltpu.VMEM((len(steps), slots, HEAD_DIM), jnp.bfloat16),
            pltpu.VMEM((len(steps), slots, ROPE), jnp.bfloat16),
            pltpu.VMEM(w_absorb_k.shape, jnp.bfloat16),
            pltpu.SemaphoreType.DMA((3,)),
        ],
        compiler_params=pltpu.CompilerParams(vmem_limit_bytes=32 * 1024 * 1024),
        cost_estimate=pl.CostEstimate(
            flops=len(units) * 256 * 1024 * 512 * 2,
            bytes_accessed=3 * 1024 * 1024,
            transcendentals=0,
        ),
        name=name,
    )(*(pltpu.with_memory_space_constraint(x, pltpu.HBM) for x in (q_nope, q_rope, w_absorb_k)))


def attend_unit(query, keys_ref, count, first_step):
    rows = query.shape[0]
    keys = keys_ref[...]
    capacity = keys.shape[1]
    scores = jnp.dot(query, keys, preferred_element_type=jnp.float32)
    position = lax.broadcasted_iota(jnp.int32, (rows, capacity), 1)
    step = first_step + lax.broadcasted_iota(jnp.int32, (rows, 1), 0) % UNIT // 8
    scores = jnp.where(position < count + step + 1, scores * score_scale, HIDDEN)
    peak = jnp.max(scores, axis=1, keepdims=True)
    spread = jnp.exp(scores - peak)
    total = jnp.sum(spread, axis=1, keepdims=True)
    weights = (spread * (1.0 / total)).astype(jnp.bfloat16)
    mixed = lax.dot_general(
        weights, keys[:LATENT], (((1,), (1,)), ((), ())), preferred_element_type=jnp.float32
    )
    return mixed.astype(jnp.bfloat16)


def place_recent(keys_ref, recent, count):
    capacity = keys_ref.shape[1]
    start = jnp.minimum(count // LANES * LANES, capacity - 2 * LANES)
    start = pl.multiple_of(start, LANES)
    steps = recent.shape[0]
    lane = start + lax.broadcasted_iota(jnp.int32, (steps, 2 * LANES), 1)
    row = lax.broadcasted_iota(jnp.int32, (steps, 2 * LANES), 0)
    chosen = jnp.where(lane == count + row, 1.0, 0.0).astype(jnp.bfloat16)
    fresh = lax.dot_general(
        recent, chosen, (((0,), (0,)), ((), ())), preferred_element_type=jnp.float32
    )
    window = keys_ref[:, pl.ds(start, 2 * LANES)].astype(jnp.float32)
    lane = start + lax.broadcasted_iota(jnp.int32, window.shape, 1)
    window = jnp.where((lane >= count) & (lane < count + steps), fresh, window)
    keys_ref[:, pl.ds(start, 2 * LANES)] = window.astype(jnp.bfloat16)


def unit_rows(got_ref, at):
    columns = got_ref.shape[0]
    return got_ref[:, pl.ds(at, UNIT), :].reshape(columns * UNIT, LANES)


def unit_latent(got_ref, at):
    return [unit_rows(got_ref, at + chunk * UNIT) for chunk in range(CHUNKS)]


def put_unit(out_ref, at, mixed):
    columns = out_ref.shape[0]
    mixed = mixed.reshape(columns, UNIT, LATENT)
    for chunk in range(CHUNKS):
        out_ref[:, pl.ds(at + chunk * UNIT, UNIT), :] = mixed[
            :, :, chunk * LANES : (chunk + 1) * LANES
        ]


def attend_kernel(plan, counts_ref, got_ref, cache_ref, recent_ref, out_ref, keys_ref, sems):
    units = sum(len(group) for group in plan)
    copies = [
        pltpu.make_async_copy(cache_ref.at[place], keys_ref.at[place], sems.at[place])
        for place in range(len(plan))
    ]
    for copy in copies:
        copy.start()
    for place, group in enumerate(plan):
        copies[place].wait()
        count = counts_ref[place]
        keys = keys_ref.at[place]
        place_recent(keys, recent_ref[place], count)
        for unit, first_step in group:
            at = unit * CHUNKS * UNIT
            rope = unit_rows(got_ref, (units * CHUNKS + unit // 2) * UNIT)
            rope = rope[:, unit % 2 * ROPE : unit % 2 * ROPE + ROPE]
            query = jnp.concatenate(unit_latent(got_ref, at) + [rope], axis=1)
            put_unit(out_ref, at, attend_unit(query, keys, count, first_step))


def attend(got, cache, recent, counts, plan, name):
    columns = got.shape[0]
    units = sum(len(group) for group in plan)
    places = len(plan)
    vmem = pl.BlockSpec(memory_space=pltpu.VMEM)
    return pl.pallas_call(
        functools.partial(attend_kernel, plan),
        out_shape=pltpu.HBM((columns, units * CHUNKS * UNIT, LANES), jnp.bfloat16),
        in_specs=[
            pl.BlockSpec(memory_space=pltpu.SMEM),
            vmem,
            pl.BlockSpec(memory_space=pltpu.HBM),
            vmem,
        ],
        out_specs=vmem,
        scratch_shapes=[
            pltpu.VMEM((places,) + cache.shape[1:], jnp.bfloat16),
            pltpu.SemaphoreType.DMA((places,)),
        ],
        compiler_params=pltpu.CompilerParams(vmem_limit_bytes=32 * 1024 * 1024),
        cost_estimate=pl.CostEstimate(
            flops=units * 256 * 1024 * 1152 * 2,
            bytes_accessed=units * 2 * 1024 * 1024,
            transcendentals=units * 256 * 1024,
        ),
        name=name,
    )(counts, got, cache, recent)


def project_unit(got_ref, at, w_ref):
    columns = got_ref.shape[0]
    heads = w_ref.shape[0]
    latent = jnp.concatenate(unit_latent(got_ref, at), axis=1)
    row_head = lax.broadcasted_iota(jnp.int32, (columns * UNIT, HEAD_DIM), 0) % heads
    result = jnp.zeros((columns * UNIT, HEAD_DIM), jnp.float32)
    for head in range(0, heads, 2):
        pair = jnp.concatenate([w_ref[head], w_ref[head + 1]], axis=1)
        product = jnp.dot(latent, pair, preferred_element_type=jnp.float32)
        result = jnp.where(row_head == head, product[:, :HEAD_DIM], result)
        result = jnp.where(row_head == head + 1, product[:, HEAD_DIM:], result)
    result = result.reshape(columns, 2, 8, HEAD_DIM)
    return result[:, 0], result[:, 1]


def join_places(near, far):
    rows = jnp.concatenate([near, far], axis=1).astype(jnp.bfloat16)
    return rows.reshape(rows.shape[0] * UNIT, HEAD_DIM)


def project_held_kernel(got_ref, w_ref, out_ref):
    span = CHUNKS * UNIT
    near = project_unit(got_ref, 0, w_ref)
    far = project_unit(got_ref, span, w_ref)
    late = project_unit(got_ref, 2 * span, w_ref)
    for step in range(2):
        out_ref[step] = join_places(near[step], far[step])
        out_ref[2 + step] = join_places(jnp.zeros_like(late[step]), late[step])


def project_moved_kernel(got_ref, w_ref, part_ref, out_ref):
    columns = got_ref.shape[0]
    near = project_unit(got_ref, 0, w_ref)
    for step in range(2):
        far = split_places(part_ref[2 + step], columns)[1]
        out_ref[step] = part_ref[step]
        out_ref[2 + step] = join_places(near[step], far)


def project(kernel, operands, units, name):
    columns = operands[0].shape[0]
    return pl.pallas_call(
        kernel,
        out_shape=jax.ShapeDtypeStruct((4, columns * UNIT, HEAD_DIM), jnp.bfloat16),
        compiler_params=pltpu.CompilerParams(vmem_limit_bytes=16 * 1024 * 1024),
        cost_estimate=pl.CostEstimate(
            flops=units * 256 * 1024 * 512 * 2, bytes_accessed=2 * 1024 * 1024, transcendentals=0
        ),
        name=name,
    )(*operands)


def shifted(value, shift, sign):
    count = lax.axis_size("grp")

    def along(steps):
        pairs = [(source, (source + steps) % count) for source in range(count)]
        return lambda given: lax.ppermute(given, "grp", pairs)

    branches = [along(sign * steps) for steps in range(1, count)]
    return lax.switch(shift - 1, branches, value)


def exchanged(value):
    return lax.all_to_all(value, "head", split_axis=0, concat_axis=0, tiled=True)


def body(q_nope, q_rope, w_absorb_k, w_absorb_v, latent_cache, new_latent, lengths, moves):
    steps, slots, heads, _ = q_nope.shape
    holders, capacity, entries = latent_cache.shape
    columns = lax.axis_size("head")
    shift = moves[0, 0]
    first_slot = (lax.axis_index("grp") * columns + lax.axis_index("head")) * holders
    counts = lax.dynamic_slice_in_dim(lengths, first_slot, holders)

    q_nope = q_nope.reshape(steps, slots * heads, HEAD_DIM)
    q_rope = q_rope.reshape(steps, slots * heads, ROPE)
    cache = jnp.swapaxes(latent_cache, 1, 2)
    recent = jnp.swapaxes(new_latent, 0, 1)

    moved_out = absorb(q_nope, q_rope, w_absorb_k, columns, (2, 3), [(2, 0)], "absorb_moved")
    held_out = absorb(
        q_nope, q_rope, w_absorb_k, columns, (0, 1, 2, 3), [(0, 0), (0, 1), (2, 1)], "absorb_held"
    )
    moved_in = exchanged(moved_out)
    fresh = shifted(new_latent[2:, 0], shift, -1)
    held_out, fresh = lax.optimization_barrier((held_out, fresh))
    held_in = exchanged(held_out)
    moved_recent = jnp.concatenate([recent[:1, :2], fresh[None]], axis=1)
    moved_in = shifted(moved_in, shift, -1)
    moved_mixed = attend(moved_in, cache, moved_recent, counts, [[(0, 2)]], "attend_moved")
    held_mixed = attend(
        held_in, cache, recent, counts, [[(0, 0)], [(1, 0), (2, 2)]], "attend_held"
    )
    held_mixed, moved_mixed = lax.optimization_barrier((held_mixed, moved_mixed))
    held_back = exchanged(held_mixed)
    moved_back = shifted(moved_mixed, shift, 1)
    moved_back = exchanged(moved_back)
    part = project(project_held_kernel, (held_back, w_absorb_v), 3, "project_held")
    out = project(project_moved_kernel, (moved_back, w_absorb_v, part), 1, "project_moved")
    return out.reshape(steps, slots, heads, HEAD_DIM)


def solution(mesh):
    placed = (
        P(None, "grp", "head", None),
        P(None, "grp", "head", None),
        P("head", None, None),
        P("head", None, None),
        P(("grp", "head"), None, None),
        P(None, ("grp", "head"), None),
        P(),
        P("head", None),
    )
    return jax.shard_map(
        body, mesh=mesh, in_specs=placed, out_specs=P(None, "grp", "head", None), check_vma=False
    )
```

```python
import functools
import math

import jax
import jax.numpy as jnp
from jax import lax
from jax.experimental import pallas as pl
from jax.experimental.pallas import tpu as pltpu
from jax.sharding import PartitionSpec as P

HEAD_DIM = 128
ROPE = 64
LATENT = 512
LANES = 128
CHUNKS = LATENT // LANES
UNIT = 16
MOVED_ROWS = CHUNKS * UNIT + UNIT // 2
HIDDEN = -1e30
LOG2_E = 1.4426950408889634

yarn_gain = (0.1 * math.log(40.0) + 1.0) ** 2
score_scale = yarn_gain / math.sqrt(HEAD_DIM + ROPE)


def split_places(rows, columns):
    wide = rows.astype(jnp.float32).reshape(columns, 2, 8, rows.shape[-1])
    return wide[:, 0], wide[:, 1]


def spread_heads(rows, heads):
    columns = rows.shape[0]
    lane_head = lax.broadcasted_iota(jnp.int32, rows.shape, 1) % heads
    pieces = [
        jnp.where(lane_head == head, rows, 0.0)
        .astype(jnp.bfloat16)
        .reshape(columns * UNIT, HEAD_DIM)
        for head in range(heads)
    ]
    return jnp.concatenate(pieces, axis=1)


def absorb_kernel(steps, units, q_hbm, r_hbm, w_hbm, out_ref, q_ref, r_ref, w_ref, sems):
    columns = out_ref.shape[0]
    heads = w_ref.shape[0]
    first = steps[0]
    copies = [
        pltpu.make_async_copy(q_hbm.at[pl.ds(first, len(steps))], q_ref, sems.at[0]),
        pltpu.make_async_copy(r_hbm.at[pl.ds(first, len(steps))], r_ref, sems.at[1]),
        pltpu.make_async_copy(w_hbm, w_ref, sems.at[2]),
    ]
    for copy in copies:
        copy.start()
    copies[0].wait()
    nope = {step: split_places(q_ref[step - first], columns) for step in steps}
    copies[1].wait()
    rope = {step: split_places(r_ref[step - first], columns) for step in steps}

    def unit_of(parts, begin, place):
        return jnp.concatenate([parts[begin][place], parts[begin + 1][place]], axis=1)

    blank = jnp.zeros((columns, UNIT, ROPE), jnp.float32)
    if len(units) == 1:
        begin, place = units[0]
        both = jnp.concatenate([rope[begin][place], rope[begin + 1][place]], axis=2)
        out_ref[:, pl.ds(CHUNKS * UNIT, UNIT // 2), :] = both.astype(jnp.bfloat16)
    for number in range(0, len(units) if len(units) > 1 else 0, 2):
        pair = [unit_of(rope, *unit) for unit in units[number : number + 2]] + [blank]
        at = (len(units) * CHUNKS + number // 2) * UNIT
        both = jnp.concatenate(pair[:2], axis=2).astype(jnp.bfloat16)
        out_ref[:, pl.ds(at, UNIT), :] = both
    copies[2].wait()
    weights = w_ref[...].reshape(heads * HEAD_DIM, LATENT)
    for number, unit in enumerate(units):
        spread = spread_heads(unit_of(nope, *unit), heads)
        latent = jnp.dot(spread, weights, preferred_element_type=jnp.float32)
        put_unit(out_ref, number * CHUNKS * UNIT, latent.astype(jnp.bfloat16))


def absorb(q_nope, q_rope, w_absorb_k, columns, steps, units, name):
    high = MOVED_ROWS if len(units) == 1 else (len(units) * CHUNKS + (len(units) + 1) // 2) * UNIT
    hbm = pl.BlockSpec(memory_space=pltpu.HBM)
    slots = q_nope.shape[1]
    return pl.pallas_call(
        functools.partial(absorb_kernel, steps, units),
        out_shape=pltpu.HBM((columns, high, LANES), jnp.bfloat16),
        in_specs=[hbm] * 3,
        scratch_shapes=[
            pltpu.VMEM((len(steps), slots, HEAD_DIM), jnp.bfloat16),
            pltpu.VMEM((len(steps), slots, ROPE), jnp.bfloat16),
            pltpu.VMEM(w_absorb_k.shape, jnp.bfloat16),
            pltpu.SemaphoreType.DMA((3,)),
        ],
        compiler_params=pltpu.CompilerParams(vmem_limit_bytes=32 * 1024 * 1024),
        cost_estimate=pl.CostEstimate(
            flops=len(units) * 256 * 1024 * 512 * 2,
            bytes_accessed=3 * 1024 * 1024,
            transcendentals=0,
        ),
        name=name,
    )(in_hbm(q_nope), in_hbm(q_rope), in_hbm(w_absorb_k))


def attend_unit(query, keys, live):
    scores = lax.dot_general(
        query, keys, (((1,), (1,)), ((), ())), preferred_element_type=jnp.float32
    )
    position = lax.broadcasted_iota(jnp.int32, scores.shape, 1)
    scores = jnp.where(position < live, scores, HIDDEN)
    peak = jnp.max(scores, axis=1, keepdims=True)
    spread = jnp.exp2((scores - peak) * (score_scale * LOG2_E))
    total = jnp.sum(spread, axis=1, keepdims=True)
    mixed = jnp.dot(
        spread.astype(jnp.bfloat16), keys[:, :LATENT], preferred_element_type=jnp.float32
    )
    return (mixed * (1.0 / total)).astype(jnp.bfloat16)


def place_recent(keys_ref, recent, count):
    capacity = keys_ref.shape[0]
    start = jnp.minimum(count // UNIT * UNIT, capacity - 2 * UNIT)
    start = pl.multiple_of(start, UNIT)
    window = keys_ref[pl.ds(start, 2 * UNIT), :].astype(jnp.float32)
    row = start + lax.broadcasted_iota(jnp.int32, window.shape, 0)
    for step in range(recent.shape[0]):
        window = jnp.where(row == count + step, recent[step : step + 1], window)
    keys_ref[pl.ds(start, 2 * UNIT), :] = window.astype(jnp.bfloat16)


def unit_rows(got_ref, at):
    columns = got_ref.shape[0]
    return got_ref[:, pl.ds(at, UNIT), :].reshape(columns * UNIT, LANES)


def unit_latent(got_ref, at):
    return [unit_rows(got_ref, at + chunk * UNIT) for chunk in range(CHUNKS)]


def put_unit(out_ref, at, mixed):
    columns = out_ref.shape[0]
    mixed = mixed.reshape(columns, UNIT, LATENT)
    for chunk in range(CHUNKS):
        out_ref[:, pl.ds(at + chunk * UNIT, UNIT), :] = mixed[
            :, :, chunk * LANES : (chunk + 1) * LANES
        ]


def prepare_kernel(counts_ref, cache_ref, recent_ref, keys_ref, fresh_ref):
    for place in range(cache_ref.shape[0]):
        for at in range(0, cache_ref.shape[2], LANES):
            keys_ref[place, pl.ds(at, LANES), :] = cache_ref[place, :, pl.ds(at, LANES)].T
        recent = recent_ref[place].astype(jnp.float32)
        place_recent(keys_ref.at[place], recent, counts_ref[place])
        if place == 0:
            late = jnp.concatenate([recent[2:], jnp.zeros((6, recent.shape[1]))], axis=0)
            rope = jnp.concatenate([late[:, LATENT:], jnp.zeros((8, ROPE))], axis=1)
            pieces = [late[:, at : at + LANES] for at in range(0, LATENT, LANES)] + [rope]
            pieces.append(jnp.zeros((MOVED_ROWS - 8 * len(pieces), LANES)))
            fresh_ref[0] = jnp.concatenate(pieces, axis=0).astype(jnp.bfloat16)


def prepare(counts, cache, recent):
    places, entries, capacity = cache.shape
    vmem = pl.BlockSpec(memory_space=pltpu.VMEM)
    return pl.pallas_call(
        prepare_kernel,
        out_shape=(
            pltpu.VMEM((places, capacity, entries), jnp.bfloat16),
            pltpu.HBM((1, MOVED_ROWS, LANES), jnp.bfloat16),
        ),
        in_specs=[pl.BlockSpec(memory_space=pltpu.SMEM), vmem, vmem],
        out_specs=(vmem, vmem),
        compiler_params=pltpu.CompilerParams(vmem_limit_bytes=24 * 1024 * 1024),
        cost_estimate=pl.CostEstimate(
            flops=1024 * 1024, bytes_accessed=8 * 1024 * 1024, transcendentals=0
        ),
        name="prepare",
    )(counts, cache, recent)


def step_of_row(rows, first_step):
    return first_step + lax.broadcasted_iota(jnp.int32, (rows, 1), 0) % UNIT // 8


def attend_held_kernel(counts_ref, got_ref, keys, out_hbm, out_ref, sems):
    span = CHUNKS * UNIT
    sends = []
    for unit, (place, first_step) in enumerate([(0, 0), (1, 0), (1, 2)]):
        rope = unit_rows(got_ref, (3 * CHUNKS + unit // 2) * UNIT)
        rope = rope[:, unit % 2 * ROPE : unit % 2 * ROPE + ROPE]
        latent = unit_latent(got_ref, unit * span)
        query = jnp.concatenate(latent + [rope], axis=1)
        live = counts_ref[place] + step_of_row(query.shape[0], first_step) + 1
        put_unit(out_ref, unit * span, attend_unit(query, keys[place], live))
        send = pltpu.make_async_copy(
            out_ref.at[:, pl.ds(unit * span, span), :],
            out_hbm.at[:, pl.ds(unit * span, span), :],
            sems.at[unit],
        )
        send.start()
        sends.append(send)
    for send in sends:
        send.wait()


def attend_moved_kernel(counts_ref, got_ref, keys_ref, out_ref, keys, sems):
    columns = out_ref.shape[0]
    copy = pltpu.make_async_copy(keys_ref.at[0], keys.at[0], sems.at[0])
    copy.start()
    rows = got_ref.at[pl.ds(0, columns)]
    both = rows[:, pl.ds(CHUNKS * UNIT, UNIT // 2), :].astype(jnp.float32)
    rope = jnp.concatenate([both[:, :, :ROPE], both[:, :, ROPE:]], axis=1)
    rope = rope.reshape(columns * UNIT, ROPE).astype(jnp.bfloat16)
    query = jnp.concatenate(unit_latent(rows, 0) + [rope], axis=1)
    fresh = got_ref[columns].astype(jnp.float32)
    pieces = [fresh[8 * chunk : 8 * chunk + 8] for chunk in range(CHUNKS + 1)]
    fresh = jnp.concatenate(pieces[:CHUNKS] + [pieces[CHUNKS][:, :ROPE]], axis=1)
    count = counts_ref[0]
    live = count + step_of_row(query.shape[0], 2) + 1
    copy.wait()
    place_recent(keys.at[0], fresh[:2], count + 2)
    put_unit(out_ref, 0, attend_unit(query, keys[0], live))


def in_hbm(value):
    return pltpu.with_memory_space_constraint(value, pltpu.HBM)


def attend(kernel, counts, got, keys, columns, units, name):
    vmem = pl.BlockSpec(memory_space=pltpu.VMEM)
    shape = (columns, units * CHUNKS * UNIT, LANES)
    if units > 1:
        out_spec, scratch = pl.BlockSpec(memory_space=pltpu.HBM), pltpu.VMEM(shape, jnp.bfloat16)
    else:
        out_spec, scratch = vmem, pltpu.VMEM((1,) + keys.shape[1:], jnp.bfloat16)
    return pl.pallas_call(
        kernel,
        out_shape=pltpu.HBM(shape, jnp.bfloat16),
        in_specs=[pl.BlockSpec(memory_space=pltpu.SMEM), vmem, vmem],
        out_specs=out_spec,
        scratch_shapes=[scratch, pltpu.SemaphoreType.DMA((units,))],
        compiler_params=pltpu.CompilerParams(vmem_limit_bytes=28 * 1024 * 1024),
        cost_estimate=pl.CostEstimate(
            flops=units * 256 * 1024 * 1152 * 2,
            bytes_accessed=units * 2 * 1024 * 1024,
            transcendentals=units * 256 * 1024,
        ),
        name=name,
    )(counts, got, keys)


def project_unit(got_ref, at, w_ref):
    columns = got_ref.shape[0]
    heads = w_ref.shape[0]
    latent = jnp.concatenate(unit_latent(got_ref, at), axis=1)
    row_head = lax.broadcasted_iota(jnp.int32, (columns * UNIT, HEAD_DIM), 0) % heads
    result = jnp.zeros((columns * UNIT, HEAD_DIM), jnp.float32)
    for head in range(0, heads, 2):
        pair = jnp.concatenate([w_ref[head], w_ref[head + 1]], axis=1)
        product = jnp.dot(latent, pair, preferred_element_type=jnp.float32)
        result = jnp.where(row_head == head, product[:, :HEAD_DIM], result)
        result = jnp.where(row_head == head + 1, product[:, HEAD_DIM:], result)
    result = result.reshape(columns, 2, 8, HEAD_DIM)
    return result[:, 0], result[:, 1]


def join_places(near, far):
    rows = jnp.concatenate([near, far], axis=1).astype(jnp.bfloat16)
    return rows.reshape(rows.shape[0] * UNIT, HEAD_DIM)


def project_held_kernel(got_ref, w_ref, out_ref):
    span = CHUNKS * UNIT
    near = project_unit(got_ref, 0, w_ref)
    far = project_unit(got_ref, span, w_ref)
    late = project_unit(got_ref, 2 * span, w_ref)
    for step in range(2):
        out_ref[step] = join_places(near[step], far[step])
        out_ref[2 + step] = join_places(jnp.zeros_like(late[step]), late[step])


def project_moved_kernel(got_ref, w_ref, part_ref, out_ref):
    columns = got_ref.shape[0]
    near = project_unit(got_ref, 0, w_ref)
    for step in range(2):
        far = split_places(part_ref[2 + step], columns)[1]
        out_ref[step] = part_ref[step]
        out_ref[2 + step] = join_places(near[step], far)


def project(kernel, operands, units, name):
    columns = operands[0].shape[0]
    return pl.pallas_call(
        kernel,
        out_shape=jax.ShapeDtypeStruct((4, columns * UNIT, HEAD_DIM), jnp.bfloat16),
        compiler_params=pltpu.CompilerParams(vmem_limit_bytes=16 * 1024 * 1024),
        cost_estimate=pl.CostEstimate(
            flops=units * 256 * 1024 * 512 * 2, bytes_accessed=2 * 1024 * 1024, transcendentals=0
        ),
        name=name,
    )(*operands)


def shifted(value, shift, sign):
    count = lax.axis_size("grp")

    def along(steps):
        pairs = [(source, (source + steps) % count) for source in range(count)]
        return lambda given: lax.ppermute(given, "grp", pairs)

    branches = [along(sign * steps) for steps in range(1, count)]
    return lax.switch(shift - 1, branches, value)


def exchanged(value):
    return lax.all_to_all(value, "head", split_axis=0, concat_axis=0, tiled=True)


def body(q_nope, q_rope, w_absorb_k, w_absorb_v, latent_cache, new_latent, lengths, moves):
    steps, slots, heads, _ = q_nope.shape
    holders, capacity, entries = latent_cache.shape
    columns = lax.axis_size("head")
    shift = moves[0, 0]
    first_slot = (lax.axis_index("grp") * columns + lax.axis_index("head")) * holders
    counts = lax.dynamic_slice_in_dim(lengths, first_slot, holders)

    q_nope = q_nope.reshape(steps, slots * heads, HEAD_DIM)
    q_rope = q_rope.reshape(steps, slots * heads, ROPE)
    cache = jnp.swapaxes(latent_cache, 1, 2)
    recent = jnp.swapaxes(new_latent, 0, 1)
    moved_out = absorb(q_nope, q_rope, w_absorb_k, columns, (2, 3), [(2, 0)], "absorb_moved")
    held_out = absorb(
        q_nope, q_rope, w_absorb_k, columns, (0, 1, 2, 3), [(0, 0), (0, 1), (2, 1)], "absorb_held"
    )
    moved_in = exchanged(moved_out)
    keys, fresh = prepare(counts, cache, recent)
    moved_in = jnp.concatenate([moved_in, fresh], axis=0)
    held_out, keys, moved_in = lax.optimization_barrier((held_out, keys, moved_in))
    held_in = exchanged(held_out)
    moved_in = shifted(moved_in, shift, -1)
    held_mixed = attend(
        attend_held_kernel, counts, held_in, keys, columns, 3, "attend_held"
    )
    moved_in, held_mixed = lax.optimization_barrier((moved_in, held_mixed))
    held_back = exchanged(held_mixed)
    moved_mixed = attend(
        attend_moved_kernel, counts, moved_in, keys, columns, 1, "attend_moved"
    )
    moved_back = exchanged(shifted(moved_mixed, shift, 1))
    part = project(project_held_kernel, (held_back, w_absorb_v), 3, "project_held")
    out = project(project_moved_kernel, (moved_back, w_absorb_v, part), 1, "project_moved")
    return out.reshape(steps, slots, heads, HEAD_DIM)


def solution(mesh):
    placed = (
        P(None, "grp", "head", None),
        P(None, "grp", "head", None),
        P("head", None, None),
        P("head", None, None),
        P(("grp", "head"), None, None),
        P(None, ("grp", "head"), None),
        P(),
        P("head", None),
    )
    return jax.shard_map(
        body, mesh=mesh, in_specs=placed, out_specs=P(None, "grp", "head", None), check_vma=False
    )
```

```python
import functools
import math

import jax
import jax.numpy as jnp
from jax import lax
from jax.experimental import pallas as pl
from jax.experimental.pallas import tpu as pltpu
from jax.sharding import PartitionSpec as P

HEAD_DIM = 128
ROPE = 64
LATENT = 512
LANES = 128
CHUNKS = LATENT // LANES
UNIT = 16
MOVED_ROWS = CHUNKS * UNIT + UNIT // 2
PARTS = 4
HIDDEN = -1e30
LOG2_E = 1.4426950408889634

yarn_gain = (0.1 * math.log(40.0) + 1.0) ** 2
score_scale = yarn_gain / math.sqrt(HEAD_DIM + ROPE)


def split_places(rows, columns):
    wide = rows.astype(jnp.float32).reshape(columns, 2, 8, rows.shape[-1])
    return wide[:, 0], wide[:, 1]


def spread_heads(rows, heads):
    columns = rows.shape[0]
    lane_head = lax.broadcasted_iota(jnp.int32, rows.shape, 1) % heads
    pieces = [
        jnp.where(lane_head == head, rows, 0.0)
        .astype(jnp.bfloat16)
        .reshape(columns * UNIT, HEAD_DIM)
        for head in range(heads)
    ]
    return jnp.concatenate(pieces, axis=1)


def absorb_kernel(steps, units, q_hbm, r_hbm, w_hbm, out_ref, q_ref, r_ref, w_ref, sems):
    columns = out_ref.shape[0]
    heads = w_ref.shape[0]
    first = steps[0]
    copies = [
        pltpu.make_async_copy(q_hbm.at[pl.ds(first, len(steps))], q_ref, sems.at[0]),
        pltpu.make_async_copy(r_hbm.at[pl.ds(first, len(steps))], r_ref, sems.at[1]),
    ]
    step = heads // PARTS
    for part in range(PARTS):
        piece = pl.ds(part * step, step)
        copies.append(
            pltpu.make_async_copy(w_hbm.at[piece], w_ref.at[piece], sems.at[2 + part])
        )
    for copy in copies:
        copy.start()
    copies[0].wait()
    nope = {step: split_places(q_ref[step - first], columns) for step in steps}
    copies[1].wait()
    rope = {step: split_places(r_ref[step - first], columns) for step in steps}

    def unit_of(parts, begin, place):
        return jnp.concatenate([parts[begin][place], parts[begin + 1][place]], axis=1)

    at = len(units) * CHUNKS * UNIT
    if len(units) > 1:
        pair = [unit_of(rope, *unit) for unit in units[:2]]
        both = jnp.concatenate(pair, axis=2).astype(jnp.bfloat16)
        out_ref[:, pl.ds(at, UNIT), :] = both
        at += UNIT
    begin, place = units[-1]
    both = jnp.concatenate([rope[begin][place], rope[begin + 1][place]], axis=2)
    out_ref[:, pl.ds(at, UNIT // 2), :] = both.astype(jnp.bfloat16)
    spreads = [spread_heads(unit_of(nope, *unit), heads) for unit in units]
    spread = jnp.concatenate(spreads, axis=0)
    latent = None
    step = heads // PARTS
    for part in range(PARTS):
        copies[2 + part].wait()
        weights = w_ref[pl.ds(part * step, step)].reshape(step * HEAD_DIM, LATENT)
        rows = spread[:, part * step * HEAD_DIM : (part + 1) * step * HEAD_DIM]
        term = jnp.dot(rows, weights, preferred_element_type=jnp.float32)
        latent = term if latent is None else latent + term
    latent = latent.astype(jnp.bfloat16)
    for number in range(len(units)):
        rows = latent[number * columns * UNIT : (number + 1) * columns * UNIT]
        put_unit(out_ref, number * CHUNKS * UNIT, rows)


def absorb(q_nope, q_rope, w_absorb_k, columns, steps, units, name):
    high = len(units) * (CHUNKS * UNIT + UNIT // 2)
    hbm = pl.BlockSpec(memory_space=pltpu.HBM)
    slots = q_nope.shape[1]
    return pl.pallas_call(
        functools.partial(absorb_kernel, steps, units),
        out_shape=pltpu.HBM((columns, high, LANES), jnp.bfloat16),
        in_specs=[hbm] * 3,
        scratch_shapes=[
            pltpu.VMEM((len(steps), slots, HEAD_DIM), jnp.bfloat16),
            pltpu.VMEM((len(steps), slots, ROPE), jnp.bfloat16),
            pltpu.VMEM(w_absorb_k.shape, jnp.bfloat16),
            pltpu.SemaphoreType.DMA((2 + PARTS,)),
        ],
        compiler_params=pltpu.CompilerParams(vmem_limit_bytes=32 * 1024 * 1024),
        cost_estimate=pl.CostEstimate(
            flops=len(units) * 256 * 1024 * 512 * 2,
            bytes_accessed=3 * 1024 * 1024,
            transcendentals=0,
        ),
        name=name,
    )(in_hbm(q_nope), in_hbm(q_rope), in_hbm(w_absorb_k))


def attend_unit(query, keys, live):
    scores = lax.dot_general(
        query, keys, (((1,), (1,)), ((), ())), preferred_element_type=jnp.float32
    )
    position = lax.broadcasted_iota(jnp.int32, scores.shape, 1)
    scores = jnp.where(position < live, scores, HIDDEN)
    peak = jnp.max(scores, axis=1, keepdims=True)
    spread = jnp.exp2((scores - peak) * (score_scale * LOG2_E))
    total = jnp.sum(spread, axis=1, keepdims=True)
    mixed = jnp.dot(
        spread.astype(jnp.bfloat16), keys[:, :LATENT], preferred_element_type=jnp.float32
    )
    return (mixed * (1.0 / total)).astype(jnp.bfloat16)


def place_recent(keys_ref, recent, count):
    capacity = keys_ref.shape[0]
    start = jnp.minimum(count // UNIT * UNIT, capacity - 2 * UNIT)
    start = pl.multiple_of(start, UNIT)
    window = keys_ref[pl.ds(start, 2 * UNIT), :].astype(jnp.float32)
    row = start + lax.broadcasted_iota(jnp.int32, window.shape, 0)
    for step in range(recent.shape[0]):
        window = jnp.where(row == count + step, recent[step : step + 1], window)
    keys_ref[pl.ds(start, 2 * UNIT), :] = window.astype(jnp.bfloat16)


def unit_rows(got_ref, at):
    columns = got_ref.shape[0]
    return got_ref[:, pl.ds(at, UNIT), :].reshape(columns * UNIT, LANES)


def unit_latent(got_ref, at):
    return [unit_rows(got_ref, at + chunk * UNIT) for chunk in range(CHUNKS)]


def put_unit(out_ref, at, mixed):
    columns = out_ref.shape[0]
    mixed = mixed.reshape(columns, UNIT, LATENT)
    for chunk in range(CHUNKS):
        out_ref[:, pl.ds(at + chunk * UNIT, UNIT), :] = mixed[
            :, :, chunk * LANES : (chunk + 1) * LANES
        ]


def prepare_kernel(counts_ref, cache_ref, recent_ref, keys_ref, fresh_ref):
    for place in range(cache_ref.shape[0]):
        for at in range(0, cache_ref.shape[2], LANES):
            keys_ref[place, pl.ds(at, LANES), :] = cache_ref[place, :, pl.ds(at, LANES)].T
        recent = recent_ref[place].astype(jnp.float32)
        place_recent(keys_ref.at[place], recent, counts_ref[place])
        if place == 0:
            late = jnp.concatenate([recent[2:], jnp.zeros((6, recent.shape[1]))], axis=0)
            rope = jnp.concatenate([late[:, LATENT:], jnp.zeros((8, ROPE))], axis=1)
            pieces = [late[:, at : at + LANES] for at in range(0, LATENT, LANES)] + [rope]
            pieces.append(jnp.zeros((MOVED_ROWS - 8 * len(pieces), LANES)))
            fresh_ref[0] = jnp.concatenate(pieces, axis=0).astype(jnp.bfloat16)


def prepare(counts, cache, recent):
    places, entries, capacity = cache.shape
    vmem = pl.BlockSpec(memory_space=pltpu.VMEM)
    return pl.pallas_call(
        prepare_kernel,
        out_shape=(
            pltpu.VMEM((places, capacity, entries), jnp.bfloat16),
            pltpu.HBM((1, MOVED_ROWS, LANES), jnp.bfloat16),
        ),
        in_specs=[pl.BlockSpec(memory_space=pltpu.SMEM), vmem, vmem],
        out_specs=(vmem, vmem),
        compiler_params=pltpu.CompilerParams(vmem_limit_bytes=24 * 1024 * 1024),
        cost_estimate=pl.CostEstimate(
            flops=1024 * 1024, bytes_accessed=8 * 1024 * 1024, transcendentals=0
        ),
        name="prepare",
    )(counts, cache, recent)


def step_of_row(rows, first_step):
    return first_step + lax.broadcasted_iota(jnp.int32, (rows, 1), 0) % UNIT // 8


def packed_rope(got_ref, at):
    columns = got_ref.shape[0]
    both = got_ref[:, pl.ds(at, UNIT // 2), :].astype(jnp.float32)
    rope = jnp.concatenate([both[:, :, :ROPE], both[:, :, ROPE:]], axis=1)
    return rope.reshape(columns * UNIT, ROPE).astype(jnp.bfloat16)


def attend_held_kernel(counts_ref, got_ref, keys, out_hbm, out_ref, sems):
    span = CHUNKS * UNIT
    pair = unit_rows(got_ref, 3 * span)
    ropes = [pair[:, :ROPE], pair[:, ROPE:], packed_rope(got_ref, 3 * span + UNIT)]
    sends = []
    for place, units in enumerate([[(0, 0)], [(1, 0), (2, 2)]]):
        queries = []
        lives = []
        for unit, first_step in units:
            latent = unit_latent(got_ref, unit * span)
            queries.append(jnp.concatenate(latent + [ropes[unit]], axis=1))
            rows = queries[-1].shape[0]
            lives.append(counts_ref[place] + step_of_row(rows, first_step) + 1)
        query = jnp.concatenate(queries, axis=0)
        mixed = attend_unit(query, keys[place], jnp.concatenate(lives, axis=0))
        for number, (unit, _) in enumerate(units):
            put_unit(out_ref, unit * span, mixed[number * rows : (number + 1) * rows])
            send = pltpu.make_async_copy(
                out_ref.at[:, pl.ds(unit * span, span), :],
                out_hbm.at[:, pl.ds(unit * span, span), :],
                sems.at[unit],
            )
            send.start()
            sends.append(send)
    for send in sends:
        send.wait()


def attend_moved_kernel(counts_ref, got_ref, keys_ref, out_ref, keys, sems):
    columns = out_ref.shape[0]
    copy = pltpu.make_async_copy(keys_ref.at[0], keys.at[0], sems.at[0])
    copy.start()
    rows = got_ref.at[pl.ds(0, columns)]
    query = jnp.concatenate(unit_latent(rows, 0) + [packed_rope(rows, CHUNKS * UNIT)], axis=1)
    fresh = got_ref[columns].astype(jnp.float32)
    pieces = [fresh[8 * chunk : 8 * chunk + 8] for chunk in range(CHUNKS + 1)]
    fresh = jnp.concatenate(pieces[:CHUNKS] + [pieces[CHUNKS][:, :ROPE]], axis=1)
    count = counts_ref[0]
    live = count + step_of_row(query.shape[0], 2) + 1
    copy.wait()
    place_recent(keys.at[0], fresh[:2], count + 2)
    put_unit(out_ref, 0, attend_unit(query, keys[0], live))


def in_hbm(value):
    return pltpu.with_memory_space_constraint(value, pltpu.HBM)


def attend(kernel, counts, got, keys, columns, units, name):
    vmem = pl.BlockSpec(memory_space=pltpu.VMEM)
    shape = (columns, units * CHUNKS * UNIT, LANES)
    if units > 1:
        out_spec, scratch = pl.BlockSpec(memory_space=pltpu.HBM), pltpu.VMEM(shape, jnp.bfloat16)
    else:
        out_spec, scratch = vmem, pltpu.VMEM((1,) + keys.shape[1:], jnp.bfloat16)
    return pl.pallas_call(
        kernel,
        out_shape=pltpu.HBM(shape, jnp.bfloat16),
        in_specs=[pl.BlockSpec(memory_space=pltpu.SMEM), vmem, vmem],
        out_specs=out_spec,
        scratch_shapes=[scratch, pltpu.SemaphoreType.DMA((units,))],
        compiler_params=pltpu.CompilerParams(vmem_limit_bytes=28 * 1024 * 1024),
        cost_estimate=pl.CostEstimate(
            flops=units * 256 * 1024 * 1152 * 2,
            bytes_accessed=units * 2 * 1024 * 1024,
            transcendentals=units * 256 * 1024,
        ),
        name=name,
    )(counts, got, keys)


def project_unit(got_ref, at, w_ref):
    columns = got_ref.shape[0]
    heads = w_ref.shape[0]
    latent = jnp.concatenate(unit_latent(got_ref, at), axis=1)
    row_head = lax.broadcasted_iota(jnp.int32, (columns * UNIT, HEAD_DIM), 0) % heads
    result = jnp.zeros((columns * UNIT, HEAD_DIM), jnp.float32)
    for head in range(0, heads, 2):
        pair = jnp.concatenate([w_ref[head], w_ref[head + 1]], axis=1)
        product = jnp.dot(latent, pair, preferred_element_type=jnp.float32)
        result = jnp.where(row_head == head, product[:, :HEAD_DIM], result)
        result = jnp.where(row_head == head + 1, product[:, HEAD_DIM:], result)
    result = result.reshape(columns, 2, 8, HEAD_DIM)
    return result[:, 0], result[:, 1]


def join_places(near, far):
    rows = jnp.concatenate([near, far], axis=1).astype(jnp.bfloat16)
    return rows.reshape(rows.shape[0] * UNIT, HEAD_DIM)


def project_held_kernel(got_ref, w_ref, out_ref):
    span = CHUNKS * UNIT
    near = project_unit(got_ref, 0, w_ref)
    far = project_unit(got_ref, span, w_ref)
    late = project_unit(got_ref, 2 * span, w_ref)
    for step in range(2):
        out_ref[step] = join_places(near[step], far[step])
        out_ref[2 + step] = join_places(jnp.zeros_like(late[step]), late[step])


def project_moved_kernel(got_ref, w_ref, part_ref, out_ref):
    columns = got_ref.shape[0]
    near = project_unit(got_ref, 0, w_ref)
    for step in range(2):
        far = split_places(part_ref[2 + step], columns)[1]
        out_ref[step] = part_ref[step]
        out_ref[2 + step] = join_places(near[step], far)


def project(kernel, operands, units, name):
    columns = operands[0].shape[0]
    return pl.pallas_call(
        kernel,
        out_shape=jax.ShapeDtypeStruct((4, columns * UNIT, HEAD_DIM), jnp.bfloat16),
        compiler_params=pltpu.CompilerParams(vmem_limit_bytes=16 * 1024 * 1024),
        cost_estimate=pl.CostEstimate(
            flops=units * 256 * 1024 * 512 * 2, bytes_accessed=2 * 1024 * 1024, transcendentals=0
        ),
        name=name,
    )(*operands)


def shifted(value, shift, sign):
    count = lax.axis_size("grp")

    def along(steps):
        pairs = [(source, (source + steps) % count) for source in range(count)]
        return lambda given: lax.ppermute(given, "grp", pairs)

    branches = [along(sign * steps) for steps in range(1, count)]
    return lax.switch(shift - 1, branches, value)


def exchanged(value):
    return lax.all_to_all(value, "head", split_axis=0, concat_axis=0, tiled=True)


def body(q_nope, q_rope, w_absorb_k, w_absorb_v, latent_cache, new_latent, lengths, moves):
    steps, slots, heads, _ = q_nope.shape
    holders, capacity, entries = latent_cache.shape
    columns = lax.axis_size("head")
    shift = moves[0, 0]
    first_slot = (lax.axis_index("grp") * columns + lax.axis_index("head")) * holders
    counts = lax.dynamic_slice_in_dim(lengths, first_slot, holders)

    q_nope = q_nope.reshape(steps, slots * heads, HEAD_DIM)
    q_rope = q_rope.reshape(steps, slots * heads, ROPE)
    cache = jnp.swapaxes(latent_cache, 1, 2)
    recent = jnp.swapaxes(new_latent, 0, 1)
    moved_out = absorb(q_nope, q_rope, w_absorb_k, columns, (2, 3), [(2, 0)], "absorb_moved")
    held_out = absorb(
        q_nope, q_rope, w_absorb_k, columns, (0, 1, 2, 3), [(0, 0), (0, 1), (2, 1)], "absorb_held"
    )
    moved_in = exchanged(moved_out)
    keys, fresh = prepare(counts, cache, recent)
    moved_in = jnp.concatenate([moved_in, fresh], axis=0)
    held_out, keys, moved_in = lax.optimization_barrier((held_out, keys, moved_in))
    held_in = exchanged(held_out)
    moved_in = shifted(moved_in, shift, -1)
    held_mixed = attend(
        attend_held_kernel, counts, held_in, keys, columns, 3, "attend_held"
    )
    moved_in, held_mixed = lax.optimization_barrier((moved_in, held_mixed))
    held_back = exchanged(held_mixed)
    moved_mixed = attend(
        attend_moved_kernel, counts, moved_in, keys, columns, 1, "attend_moved"
    )
    moved_back = exchanged(shifted(moved_mixed, shift, 1))
    part = project(project_held_kernel, (held_back, w_absorb_v), 3, "project_held")
    out = project(project_moved_kernel, (moved_back, w_absorb_v, part), 1, "project_moved")
    return out.reshape(steps, slots, heads, HEAD_DIM)


def solution(mesh):
    placed = (
        P(None, "grp", "head", None),
        P(None, "grp", "head", None),
        P("head", None, None),
        P("head", None, None),
        P(("grp", "head"), None, None),
        P(None, ("grp", "head"), None),
        P(),
        P("head", None),
    )
    return jax.shard_map(
        body, mesh=mesh, in_specs=placed, out_specs=P(None, "grp", "head", None), check_vma=False
    )
```

```python
import functools
import math

import jax
import jax.numpy as jnp
from jax import lax
from jax.experimental import pallas as pl
from jax.experimental.pallas import tpu as pltpu
from jax.sharding import PartitionSpec as P

HEAD_DIM = 128
ROPE = 64
LATENT = 512
LANES = 128
CHUNKS = LATENT // LANES
UNIT = 16
MOVED_ROWS = CHUNKS * UNIT + UNIT // 2
PARTS = 4
HIDDEN = -1e30
LOG2_E = 1.4426950408889634

yarn_gain = (0.1 * math.log(40.0) + 1.0) ** 2
score_scale = yarn_gain / math.sqrt(HEAD_DIM + ROPE)


def split_places(rows, columns):
    wide = rows.astype(jnp.float32).reshape(columns, 2, 8, rows.shape[-1])
    return wide[:, 0], wide[:, 1]


def spread_heads(rows, heads):
    columns = rows.shape[0]
    lane_head = lax.broadcasted_iota(jnp.int32, rows.shape, 1) % heads
    pieces = [
        jnp.where(lane_head == head, rows, 0.0)
        .astype(jnp.bfloat16)
        .reshape(columns * UNIT, HEAD_DIM)
        for head in range(heads)
    ]
    return jnp.concatenate(pieces, axis=1)


def absorb_kernel(steps, units, q_hbm, r_hbm, w_hbm, out_ref, q_ref, r_ref, w_ref, sems):
    columns = out_ref.shape[0]
    heads = w_ref.shape[0]
    first = steps[0]
    copies = [
        pltpu.make_async_copy(q_hbm.at[pl.ds(first, len(steps))], q_ref, sems.at[0]),
        pltpu.make_async_copy(r_hbm.at[pl.ds(first, len(steps))], r_ref, sems.at[1]),
    ]
    step = heads // PARTS
    for part in range(PARTS):
        piece = pl.ds(part * step, step)
        copies.append(
            pltpu.make_async_copy(w_hbm.at[piece], w_ref.at[piece], sems.at[2 + part])
        )
    for copy in copies:
        copy.start()
    copies[0].wait()
    nope = {step: split_places(q_ref[step - first], columns) for step in steps}
    copies[1].wait()
    rope = {step: split_places(r_ref[step - first], columns) for step in steps}

    def unit_of(parts, begin, place):
        return jnp.concatenate([parts[begin][place], parts[begin + 1][place]], axis=1)

    at = len(units) * CHUNKS * UNIT
    if len(units) > 1:
        pair = [unit_of(rope, *unit) for unit in units[:2]]
        both = jnp.concatenate(pair, axis=2).astype(jnp.bfloat16)
        out_ref[:, pl.ds(at, UNIT), :] = both
        at += UNIT
    begin, place = units[-1]
    both = jnp.concatenate([rope[begin][place], rope[begin + 1][place]], axis=2)
    out_ref[:, pl.ds(at, UNIT // 2), :] = both.astype(jnp.bfloat16)
    spreads = [spread_heads(unit_of(nope, *unit), heads) for unit in units]
    spread = jnp.concatenate(spreads, axis=0)
    latent = None
    step = heads // PARTS
    for part in range(PARTS):
        copies[2 + part].wait()
        weights = w_ref[pl.ds(part * step, step)].reshape(step * HEAD_DIM, LATENT)
        rows = spread[:, part * step * HEAD_DIM : (part + 1) * step * HEAD_DIM]
        term = jnp.dot(rows, weights, preferred_element_type=jnp.float32)
        latent = term if latent is None else latent + term
    latent = latent.astype(jnp.bfloat16)
    for number in range(len(units)):
        rows = latent[number * columns * UNIT : (number + 1) * columns * UNIT]
        put_unit(out_ref, number * CHUNKS * UNIT, rows)


def absorb(q_nope, q_rope, w_absorb_k, columns, steps, units, name):
    high = len(units) * (CHUNKS * UNIT + UNIT // 2)
    hbm = pl.BlockSpec(memory_space=pltpu.HBM)
    slots = q_nope.shape[1]
    return pl.pallas_call(
        functools.partial(absorb_kernel, steps, units),
        out_shape=pltpu.HBM((columns, high, LANES), jnp.bfloat16),
        in_specs=[hbm] * 3,
        scratch_shapes=[
            pltpu.VMEM((len(steps), slots, HEAD_DIM), jnp.bfloat16),
            pltpu.VMEM((len(steps), slots, ROPE), jnp.bfloat16),
            pltpu.VMEM(w_absorb_k.shape, jnp.bfloat16),
            pltpu.SemaphoreType.DMA((2 + PARTS,)),
        ],
        compiler_params=pltpu.CompilerParams(vmem_limit_bytes=32 * 1024 * 1024),
        cost_estimate=pl.CostEstimate(
            flops=len(units) * 256 * 1024 * 512 * 2,
            bytes_accessed=3 * 1024 * 1024,
            transcendentals=0,
        ),
        name=name,
    )(in_hbm(q_nope), in_hbm(q_rope), in_hbm(w_absorb_k))


def scores_of(query, keys):
    return lax.dot_general(
        query, keys, (((1,), (1,)), ((), ())), preferred_element_type=jnp.float32
    )


def attend_unit(query, keys, live, scores=None):
    if scores is None:
        scores = scores_of(query, keys)
    position = lax.broadcasted_iota(jnp.int32, scores.shape, 1)
    scores = jnp.where(position < live, scores, HIDDEN)
    peak = jnp.max(scores, axis=1, keepdims=True)
    spread = jnp.exp2((scores - peak) * (score_scale * LOG2_E))
    total = jnp.sum(spread, axis=1, keepdims=True)
    mixed = jnp.dot(
        spread.astype(jnp.bfloat16), keys[:, :LATENT], preferred_element_type=jnp.float32
    )
    return (mixed * (1.0 / total)).astype(jnp.bfloat16)


def place_recent(keys_ref, recent, count):
    capacity = keys_ref.shape[0]
    start = jnp.minimum(count // UNIT * UNIT, capacity - 2 * UNIT)
    start = pl.multiple_of(start, UNIT)
    window = keys_ref[pl.ds(start, 2 * UNIT), :].astype(jnp.float32)
    row = start + lax.broadcasted_iota(jnp.int32, window.shape, 0)
    for step in range(recent.shape[0]):
        window = jnp.where(row == count + step, recent[step : step + 1], window)
    keys_ref[pl.ds(start, 2 * UNIT), :] = window.astype(jnp.bfloat16)


def unit_rows(got_ref, at):
    columns = got_ref.shape[0]
    return got_ref[:, pl.ds(at, UNIT), :].reshape(columns * UNIT, LANES)


def unit_latent(got_ref, at):
    return [unit_rows(got_ref, at + chunk * UNIT) for chunk in range(CHUNKS)]


def put_unit(out_ref, at, mixed):
    columns = out_ref.shape[0]
    mixed = mixed.reshape(columns, UNIT, LATENT)
    for chunk in range(CHUNKS):
        out_ref[:, pl.ds(at + chunk * UNIT, UNIT), :] = mixed[
            :, :, chunk * LANES : (chunk + 1) * LANES
        ]


def prepare_kernel(counts_ref, cache_ref, recent_ref, keys_ref, fresh_ref):
    for place in range(cache_ref.shape[0]):
        for at in range(0, cache_ref.shape[2], LANES):
            keys_ref[place, pl.ds(at, LANES), :] = cache_ref[place, :, pl.ds(at, LANES)].T
        recent = recent_ref[place].astype(jnp.float32)
        place_recent(keys_ref.at[place], recent, counts_ref[place])
        if place == 0:
            late = jnp.concatenate([recent[2:], jnp.zeros((6, recent.shape[1]))], axis=0)
            rope = jnp.concatenate([late[:, LATENT:], jnp.zeros((8, ROPE))], axis=1)
            pieces = [late[:, at : at + LANES] for at in range(0, LATENT, LANES)] + [rope]
            pieces.append(jnp.zeros((MOVED_ROWS - 8 * len(pieces), LANES)))
            fresh_ref[0] = jnp.concatenate(pieces, axis=0).astype(jnp.bfloat16)


def prepare(counts, cache, recent):
    places, entries, capacity = cache.shape
    vmem = pl.BlockSpec(memory_space=pltpu.VMEM)
    return pl.pallas_call(
        prepare_kernel,
        out_shape=(
            pltpu.VMEM((places, capacity, entries), jnp.bfloat16),
            pltpu.HBM((1, MOVED_ROWS, LANES), jnp.bfloat16),
        ),
        in_specs=[pl.BlockSpec(memory_space=pltpu.SMEM), vmem, vmem],
        out_specs=(vmem, vmem),
        compiler_params=pltpu.CompilerParams(vmem_limit_bytes=24 * 1024 * 1024),
        cost_estimate=pl.CostEstimate(
            flops=1024 * 1024, bytes_accessed=8 * 1024 * 1024, transcendentals=0
        ),
        name="prepare",
    )(counts, cache, recent)


def step_of_row(rows, first_step):
    return first_step + lax.broadcasted_iota(jnp.int32, (rows, 1), 0) % UNIT // 8


def packed_rope(got_ref, at):
    columns = got_ref.shape[0]
    both = got_ref[:, pl.ds(at, UNIT // 2), :].astype(jnp.float32)
    rope = jnp.concatenate([both[:, :, :ROPE], both[:, :, ROPE:]], axis=1)
    return rope.reshape(columns * UNIT, ROPE).astype(jnp.bfloat16)


def attend_held_kernel(counts_ref, got_ref, keys, out_hbm, out_ref, sems):
    span = CHUNKS * UNIT
    pair = unit_rows(got_ref, 3 * span)
    ropes = [pair[:, :ROPE], pair[:, ROPE:], packed_rope(got_ref, 3 * span + UNIT)]
    sends = []
    jobs = []
    for place, units in enumerate([[(0, 0)], [(1, 0), (2, 2)]]):
        queries = []
        lives = []
        for unit, first_step in units:
            latent = unit_latent(got_ref, unit * span)
            queries.append(jnp.concatenate(latent + [ropes[unit]], axis=1))
            rows = queries[-1].shape[0]
            lives.append(counts_ref[place] + step_of_row(rows, first_step) + 1)
        query = jnp.concatenate(queries, axis=0)
        jobs.append((place, units, query, jnp.concatenate(lives, axis=0), scores_of(query, keys[place])))
    for place, units, query, live, scores in jobs:
        mixed = attend_unit(query, keys[place], live, scores)
        for number, (unit, _) in enumerate(units):
            put_unit(out_ref, unit * span, mixed[number * rows : (number + 1) * rows])
            send = pltpu.make_async_copy(
                out_ref.at[:, pl.ds(unit * span, span), :],
                out_hbm.at[:, pl.ds(unit * span, span), :],
                sems.at[unit],
            )
            send.start()
            sends.append(send)
    for send in sends:
        send.wait()


def attend_moved_kernel(counts_ref, got_ref, keys_ref, out_ref, keys, sems):
    columns = out_ref.shape[0]
    copy = pltpu.make_async_copy(keys_ref.at[0], keys.at[0], sems.at[0])
    copy.start()
    rows = got_ref.at[pl.ds(0, columns)]
    query = jnp.concatenate(unit_latent(rows, 0) + [packed_rope(rows, CHUNKS * UNIT)], axis=1)
    fresh = got_ref[columns].astype(jnp.float32)
    pieces = [fresh[8 * chunk : 8 * chunk + 8] for chunk in range(CHUNKS + 1)]
    fresh = jnp.concatenate(pieces[:CHUNKS] + [pieces[CHUNKS][:, :ROPE]], axis=1)
    count = counts_ref[0]
    live = count + step_of_row(query.shape[0], 2) + 1
    copy.wait()
    place_recent(keys.at[0], fresh[:2], count + 2)
    put_unit(out_ref, 0, attend_unit(query, keys[0], live))


def in_hbm(value):
    return pltpu.with_memory_space_constraint(value, pltpu.HBM)


def attend(kernel, counts, got, keys, columns, units, name):
    vmem = pl.BlockSpec(memory_space=pltpu.VMEM)
    shape = (columns, units * CHUNKS * UNIT, LANES)
    if units > 1:
        out_spec, scratch = pl.BlockSpec(memory_space=pltpu.HBM), pltpu.VMEM(shape, jnp.bfloat16)
    else:
        out_spec, scratch = vmem, pltpu.VMEM((1,) + keys.shape[1:], jnp.bfloat16)
    return pl.pallas_call(
        kernel,
        out_shape=pltpu.HBM(shape, jnp.bfloat16),
        in_specs=[pl.BlockSpec(memory_space=pltpu.SMEM), vmem, vmem],
        out_specs=out_spec,
        scratch_shapes=[scratch, pltpu.SemaphoreType.DMA((units,))],
        compiler_params=pltpu.CompilerParams(vmem_limit_bytes=28 * 1024 * 1024),
        cost_estimate=pl.CostEstimate(
            flops=units * 256 * 1024 * 1152 * 2,
            bytes_accessed=units * 2 * 1024 * 1024,
            transcendentals=units * 256 * 1024,
        ),
        name=name,
    )(counts, got, keys)


def project_unit(got_ref, at, w_ref):
    columns = got_ref.shape[0]
    heads = w_ref.shape[0]
    latent = jnp.concatenate(unit_latent(got_ref, at), axis=1)
    row_head = lax.broadcasted_iota(jnp.int32, (columns * UNIT, HEAD_DIM), 0) % heads
    result = jnp.zeros((columns * UNIT, HEAD_DIM), jnp.float32)
    for head in range(0, heads, 2):
        pair = jnp.concatenate([w_ref[head], w_ref[head + 1]], axis=1)
        product = jnp.dot(latent, pair, preferred_element_type=jnp.float32)
        result = jnp.where(row_head == head, product[:, :HEAD_DIM], result)
        result = jnp.where(row_head == head + 1, product[:, HEAD_DIM:], result)
    result = result.reshape(columns, 2, 8, HEAD_DIM)
    return result[:, 0], result[:, 1]


def join_places(near, far):
    rows = jnp.concatenate([near, far], axis=1).astype(jnp.bfloat16)
    return rows.reshape(rows.shape[0] * UNIT, HEAD_DIM)


def project_held_kernel(got_ref, w_ref, out_ref):
    span = CHUNKS * UNIT
    near = project_unit(got_ref, 0, w_ref)
    far = project_unit(got_ref, span, w_ref)
    late = project_unit(got_ref, 2 * span, w_ref)
    for step in range(2):
        out_ref[step] = join_places(near[step], far[step])
        out_ref[2 + step] = join_places(jnp.zeros_like(late[step]), late[step])


def project_moved_kernel(got_ref, w_ref, part_ref, out_ref):
    columns = got_ref.shape[0]
    near = project_unit(got_ref, 0, w_ref)
    for step in range(2):
        far = split_places(part_ref[2 + step], columns)[1]
        out_ref[step] = part_ref[step]
        out_ref[2 + step] = join_places(near[step], far)


def project(kernel, operands, units, name):
    columns = operands[0].shape[0]
    return pl.pallas_call(
        kernel,
        out_shape=jax.ShapeDtypeStruct((4, columns * UNIT, HEAD_DIM), jnp.bfloat16),
        compiler_params=pltpu.CompilerParams(vmem_limit_bytes=16 * 1024 * 1024),
        cost_estimate=pl.CostEstimate(
            flops=units * 256 * 1024 * 512 * 2, bytes_accessed=2 * 1024 * 1024, transcendentals=0
        ),
        name=name,
    )(*operands)


def shifted(value, shift, sign):
    count = lax.axis_size("grp")

    def along(steps):
        pairs = [(source, (source + steps) % count) for source in range(count)]
        return lambda given: lax.ppermute(given, "grp", pairs)

    branches = [along(sign * steps) for steps in range(1, count)]
    return lax.switch(shift - 1, branches, value)


def exchanged(value):
    return lax.all_to_all(value, "head", split_axis=0, concat_axis=0, tiled=True)


def body(q_nope, q_rope, w_absorb_k, w_absorb_v, latent_cache, new_latent, lengths, moves):
    steps, slots, heads, _ = q_nope.shape
    holders, capacity, entries = latent_cache.shape
    columns = lax.axis_size("head")
    shift = moves[0, 0]
    first_slot = (lax.axis_index("grp") * columns + lax.axis_index("head")) * holders
    counts = lax.dynamic_slice_in_dim(lengths, first_slot, holders)

    q_nope = q_nope.reshape(steps, slots * heads, HEAD_DIM)
    q_rope = q_rope.reshape(steps, slots * heads, ROPE)
    cache = jnp.swapaxes(latent_cache, 1, 2)
    recent = jnp.swapaxes(new_latent, 0, 1)
    moved_out = absorb(q_nope, q_rope, w_absorb_k, columns, (2, 3), [(2, 0)], "absorb_moved")
    held_out = absorb(
        q_nope, q_rope, w_absorb_k, columns, (0, 1, 2, 3), [(0, 0), (0, 1), (2, 1)], "absorb_held"
    )
    moved_in = exchanged(moved_out)
    keys, fresh = prepare(counts, cache, recent)
    moved_in = jnp.concatenate([moved_in, fresh], axis=0)
    held_out, keys, moved_in = lax.optimization_barrier((held_out, keys, moved_in))
    held_in = exchanged(held_out)
    moved_in = shifted(moved_in, shift, -1)
    held_mixed = attend(
        attend_held_kernel, counts, held_in, keys, columns, 3, "attend_held"
    )
    moved_in, held_mixed = lax.optimization_barrier((moved_in, held_mixed))
    held_back = exchanged(held_mixed)
    moved_mixed = attend(
        attend_moved_kernel, counts, moved_in, keys, columns, 1, "attend_moved"
    )
    moved_back = exchanged(shifted(moved_mixed, shift, 1))
    part = project(project_held_kernel, (held_back, w_absorb_v), 3, "project_held")
    out = project(project_moved_kernel, (moved_back, w_absorb_v, part), 1, "project_moved")
    return out.reshape(steps, slots, heads, HEAD_DIM)


def solution(mesh):
    placed = (
        P(None, "grp", "head", None),
        P(None, "grp", "head", None),
        P("head", None, None),
        P("head", None, None),
        P(("grp", "head"), None, None),
        P(None, ("grp", "head"), None),
        P(),
        P("head", None),
    )
    return jax.shard_map(
        body, mesh=mesh, in_specs=placed, out_specs=P(None, "grp", "head", None), check_vma=False
    )
```

```python
import functools
import math

import jax
import jax.numpy as jnp
from jax import lax
from jax.experimental import pallas as pl
from jax.experimental.pallas import tpu as pltpu
from jax.sharding import PartitionSpec as P

HEAD_DIM = 128
ROPE = 64
LATENT = 512
LANES = 128
CHUNKS = LATENT // LANES
UNIT = 16
MOVED_ROWS = CHUNKS * UNIT + UNIT // 2
PARTS = 4
HIDDEN = -1e30
LOG2_E = 1.4426950408889634

yarn_gain = (0.1 * math.log(40.0) + 1.0) ** 2
score_scale = yarn_gain / math.sqrt(HEAD_DIM + ROPE)


def split_places(rows, columns):
    wide = rows.astype(jnp.float32).reshape(columns, 2, 8, rows.shape[-1])
    return wide[:, 0], wide[:, 1]


def spread_heads(rows, heads):
    columns = rows.shape[0]
    lane_head = lax.broadcasted_iota(jnp.int32, rows.shape, 1) % heads
    pieces = [
        jnp.where(lane_head == head, rows, 0.0)
        .astype(jnp.bfloat16)
        .reshape(columns * UNIT, HEAD_DIM)
        for head in range(heads)
    ]
    return jnp.concatenate(pieces, axis=1)


def absorb_kernel(steps, units, q_hbm, r_hbm, w_hbm, out_ref, q_ref, r_ref, w_ref, sems):
    columns = out_ref.shape[0]
    heads = w_ref.shape[0]
    first = steps[0]
    copies = [
        pltpu.make_async_copy(q_hbm.at[pl.ds(first, len(steps))], q_ref, sems.at[0]),
        pltpu.make_async_copy(r_hbm.at[pl.ds(first, len(steps))], r_ref, sems.at[1]),
    ]
    step = heads // PARTS
    for part in range(PARTS):
        piece = pl.ds(part * step, step)
        copies.append(
            pltpu.make_async_copy(w_hbm.at[piece], w_ref.at[piece], sems.at[2 + part])
        )
    for copy in copies:
        copy.start()
    copies[0].wait()
    nope = {step: split_places(q_ref[step - first], columns) for step in steps}
    copies[1].wait()
    rope = {step: split_places(r_ref[step - first], columns) for step in steps}

    def unit_of(parts, begin, place):
        return jnp.concatenate([parts[begin][place], parts[begin + 1][place]], axis=1)

    at = len(units) * CHUNKS * UNIT
    if len(units) > 1:
        pair = [unit_of(rope, *unit) for unit in units[:2]]
        both = jnp.concatenate(pair, axis=2).astype(jnp.bfloat16)
        out_ref[:, pl.ds(at, UNIT), :] = both
        at += UNIT
    begin, place = units[-1]
    both = jnp.concatenate([rope[begin][place], rope[begin + 1][place]], axis=2)
    out_ref[:, pl.ds(at, UNIT // 2), :] = both.astype(jnp.bfloat16)
    spreads = [spread_heads(unit_of(nope, *unit), heads) for unit in units]
    spread = jnp.concatenate(spreads, axis=0)
    latent = None
    step = heads // PARTS
    for part in range(PARTS):
        copies[2 + part].wait()
        weights = w_ref[pl.ds(part * step, step)].reshape(step * HEAD_DIM, LATENT)
        rows = spread[:, part * step * HEAD_DIM : (part + 1) * step * HEAD_DIM]
        term = jnp.dot(rows, weights, preferred_element_type=jnp.float32)
        latent = term if latent is None else latent + term
    latent = latent.astype(jnp.bfloat16)
    for number in range(len(units)):
        rows = latent[number * columns * UNIT : (number + 1) * columns * UNIT]
        put_unit(out_ref, number * CHUNKS * UNIT, rows)


def absorb(q_nope, q_rope, w_absorb_k, columns, steps, units, name):
    high = len(units) * (CHUNKS * UNIT + UNIT // 2)
    hbm = pl.BlockSpec(memory_space=pltpu.HBM)
    slots = q_nope.shape[1]
    return pl.pallas_call(
        functools.partial(absorb_kernel, steps, units),
        out_shape=pltpu.HBM((columns, high, LANES), jnp.bfloat16),
        in_specs=[hbm] * 3,
        scratch_shapes=[
            pltpu.VMEM((len(steps), slots, HEAD_DIM), jnp.bfloat16),
            pltpu.VMEM((len(steps), slots, ROPE), jnp.bfloat16),
            pltpu.VMEM(w_absorb_k.shape, jnp.bfloat16),
            pltpu.SemaphoreType.DMA((2 + PARTS,)),
        ],
        compiler_params=pltpu.CompilerParams(vmem_limit_bytes=32 * 1024 * 1024),
        cost_estimate=pl.CostEstimate(
            flops=len(units) * 256 * 1024 * 512 * 2,
            bytes_accessed=3 * 1024 * 1024,
            transcendentals=0,
        ),
        name=name,
    )(in_hbm(q_nope), in_hbm(q_rope), in_hbm(w_absorb_k))


def scores_of(query, keys):
    return lax.dot_general(
        query, keys, (((1,), (1,)), ((), ())), preferred_element_type=jnp.float32
    )


def attend_unit(query, keys, live, scores=None):
    if scores is None:
        scores = scores_of(query, keys)
    position = lax.broadcasted_iota(jnp.int32, scores.shape, 1)
    scores = jnp.where(position < live, scores, HIDDEN)
    peak = jnp.max(scores, axis=1, keepdims=True)
    spread = jnp.exp2((scores - peak) * (score_scale * LOG2_E))
    total = jnp.sum(spread, axis=1, keepdims=True)
    mixed = jnp.dot(
        spread.astype(jnp.bfloat16), keys[:, :LATENT], preferred_element_type=jnp.float32
    )
    return (mixed * (1.0 / total)).astype(jnp.bfloat16)


def place_recent(keys_ref, recent, count):
    capacity = keys_ref.shape[0]
    start = jnp.minimum(count // UNIT * UNIT, capacity - 2 * UNIT)
    start = pl.multiple_of(start, UNIT)
    window = keys_ref[pl.ds(start, 2 * UNIT), :].astype(jnp.float32)
    row = start + lax.broadcasted_iota(jnp.int32, window.shape, 0)
    for step in range(recent.shape[0]):
        window = jnp.where(row == count + step, recent[step : step + 1], window)
    keys_ref[pl.ds(start, 2 * UNIT), :] = window.astype(jnp.bfloat16)


def unit_rows(got_ref, at):
    columns = got_ref.shape[0]
    return got_ref[:, pl.ds(at, UNIT), :].reshape(columns * UNIT, LANES)


def unit_latent(got_ref, at):
    return [unit_rows(got_ref, at + chunk * UNIT) for chunk in range(CHUNKS)]


def put_unit(out_ref, at, mixed):
    columns = out_ref.shape[0]
    mixed = mixed.reshape(columns, UNIT, LATENT)
    for chunk in range(CHUNKS):
        out_ref[:, pl.ds(at + chunk * UNIT, UNIT), :] = mixed[
            :, :, chunk * LANES : (chunk + 1) * LANES
        ]


def prepare_kernel(counts_ref, cache_ref, recent_ref, keys_ref, fresh_ref):
    for place in range(cache_ref.shape[0]):
        for at in range(0, cache_ref.shape[2], LANES):
            keys_ref[place, pl.ds(at, LANES), :] = cache_ref[place, :, pl.ds(at, LANES)].T
        recent = recent_ref[place].astype(jnp.float32)
        place_recent(keys_ref.at[place], recent, counts_ref[place])
        if place == 0:
            late = jnp.concatenate([recent[2:], jnp.zeros((6, recent.shape[1]))], axis=0)
            rope = jnp.concatenate([late[:, LATENT:], jnp.zeros((8, ROPE))], axis=1)
            pieces = [late[:, at : at + LANES] for at in range(0, LATENT, LANES)] + [rope]
            pieces.append(jnp.zeros((MOVED_ROWS - 8 * len(pieces), LANES)))
            fresh_ref[0] = jnp.concatenate(pieces, axis=0).astype(jnp.bfloat16)


def prepare(counts, cache, recent):
    places, entries, capacity = cache.shape
    vmem = pl.BlockSpec(memory_space=pltpu.VMEM)
    return pl.pallas_call(
        prepare_kernel,
        out_shape=(
            pltpu.VMEM((places, capacity, entries), jnp.bfloat16),
            pltpu.HBM((1, MOVED_ROWS, LANES), jnp.bfloat16),
        ),
        in_specs=[pl.BlockSpec(memory_space=pltpu.SMEM), vmem, vmem],
        out_specs=(vmem, vmem),
        compiler_params=pltpu.CompilerParams(vmem_limit_bytes=24 * 1024 * 1024),
        cost_estimate=pl.CostEstimate(
            flops=1024 * 1024, bytes_accessed=8 * 1024 * 1024, transcendentals=0
        ),
        name="prepare",
    )(counts, cache, recent)


def step_of_row(rows, first_step):
    return first_step + lax.broadcasted_iota(jnp.int32, (rows, 1), 0) % UNIT // 8


def packed_rope(got_ref, at):
    columns = got_ref.shape[0]
    both = got_ref[:, pl.ds(at, UNIT // 2), :].astype(jnp.float32)
    rope = jnp.concatenate([both[:, :, :ROPE], both[:, :, ROPE:]], axis=1)
    return rope.reshape(columns * UNIT, ROPE).astype(jnp.bfloat16)


def attend_held_kernel(counts_ref, got_ref, keys, out_hbm, out_ref, sems):
    span = CHUNKS * UNIT
    pair = unit_rows(got_ref, 3 * span)
    ropes = [pair[:, :ROPE], pair[:, ROPE:], packed_rope(got_ref, 3 * span + UNIT)]
    sends = []
    jobs = []
    for place, units in enumerate([[(0, 0)], [(1, 0), (2, 2)]]):
        queries = []
        lives = []
        for unit, first_step in units:
            latent = unit_latent(got_ref, unit * span)
            queries.append(jnp.concatenate(latent + [ropes[unit]], axis=1))
            rows = queries[-1].shape[0]
            lives.append(counts_ref[place] + step_of_row(rows, first_step) + 1)
        query = jnp.concatenate(queries, axis=0)
        jobs.append((place, units, query, jnp.concatenate(lives, axis=0), scores_of(query, keys[place])))
    for place, units, query, live, scores in jobs:
        mixed = attend_unit(query, keys[place], live, scores)
        for number, (unit, _) in enumerate(units):
            put_unit(out_ref, unit * span, mixed[number * rows : (number + 1) * rows])
            send = pltpu.make_async_copy(
                out_ref.at[:, pl.ds(unit * span, span), :],
                out_hbm.at[:, pl.ds(unit * span, span), :],
                sems.at[unit],
            )
            send.start()
            sends.append(send)
    for send in sends:
        send.wait()


def attend_moved_kernel(counts_ref, got_ref, keys_ref, out_ref, keys, sems):
    columns = out_ref.shape[0]
    copy = pltpu.make_async_copy(keys_ref.at[0], keys.at[0], sems.at[0])
    copy.start()
    rows = got_ref.at[pl.ds(0, columns)]
    query = jnp.concatenate(unit_latent(rows, 0) + [packed_rope(rows, CHUNKS * UNIT)], axis=1)
    fresh = got_ref[columns].astype(jnp.float32)
    pieces = [fresh[8 * chunk : 8 * chunk + 8] for chunk in range(CHUNKS + 1)]
    fresh = jnp.concatenate(pieces[:CHUNKS] + [pieces[CHUNKS][:, :ROPE]], axis=1)
    count = counts_ref[0]
    live = count + step_of_row(query.shape[0], 2) + 1
    copy.wait()
    place_recent(keys.at[0], fresh[:2], count + 2)
    put_unit(out_ref, 0, attend_unit(query, keys[0], live))


def in_hbm(value):
    return pltpu.with_memory_space_constraint(value, pltpu.HBM)


def attend(kernel, counts, got, keys, columns, units, name):
    vmem = pl.BlockSpec(memory_space=pltpu.VMEM)
    shape = (columns, units * CHUNKS * UNIT, LANES)
    if units > 1:
        out_spec, scratch = pl.BlockSpec(memory_space=pltpu.HBM), pltpu.VMEM(shape, jnp.bfloat16)
    else:
        out_spec, scratch = vmem, pltpu.VMEM((1,) + keys.shape[1:], jnp.bfloat16)
    return pl.pallas_call(
        kernel,
        out_shape=pltpu.HBM(shape, jnp.bfloat16),
        in_specs=[pl.BlockSpec(memory_space=pltpu.SMEM), vmem, vmem],
        out_specs=out_spec,
        scratch_shapes=[scratch, pltpu.SemaphoreType.DMA((units,))],
        compiler_params=pltpu.CompilerParams(vmem_limit_bytes=28 * 1024 * 1024),
        cost_estimate=pl.CostEstimate(
            flops=units * 256 * 1024 * 1152 * 2,
            bytes_accessed=units * 2 * 1024 * 1024,
            transcendentals=units * 256 * 1024,
        ),
        name=name,
    )(counts, got, keys)


def project_unit(got_ref, at, w_ref):
    columns = got_ref.shape[0]
    heads = w_ref.shape[0]
    latent = jnp.concatenate(unit_latent(got_ref, at), axis=1)
    row_head = lax.broadcasted_iota(jnp.int32, (columns * UNIT, HEAD_DIM), 0) % heads
    result = jnp.zeros((columns * UNIT, HEAD_DIM), jnp.float32)
    for head in range(0, heads, 2):
        pair = jnp.concatenate([w_ref[head], w_ref[head + 1]], axis=1)
        product = jnp.dot(latent, pair, preferred_element_type=jnp.float32)
        result = jnp.where(row_head == head, product[:, :HEAD_DIM], result)
        result = jnp.where(row_head == head + 1, product[:, HEAD_DIM:], result)
    result = result.reshape(columns, 2, 8, HEAD_DIM)
    return result[:, 0], result[:, 1]


def join_places(near, far):
    rows = jnp.concatenate([near, far], axis=1).astype(jnp.bfloat16)
    return rows.reshape(rows.shape[0] * UNIT, HEAD_DIM)


def project_held_kernel(got_ref, w_ref, out_ref):
    span = CHUNKS * UNIT
    near = project_unit(got_ref, 0, w_ref)
    far = project_unit(got_ref, span, w_ref)
    late = project_unit(got_ref, 2 * span, w_ref)
    for step in range(2):
        out_ref[step] = join_places(near[step], far[step])
        out_ref[2 + step] = join_places(jnp.zeros_like(late[step]), late[step])


def project_moved_kernel(got_ref, w_ref, part_ref, out_ref):
    columns = got_ref.shape[0]
    near = project_unit(got_ref, 0, w_ref)
    for step in range(2):
        far = split_places(part_ref[2 + step], columns)[1]
        out_ref[step] = part_ref[step]
        out_ref[2 + step] = join_places(near[step], far)


def project(kernel, operands, units, name):
    columns = operands[0].shape[0]
    return pl.pallas_call(
        kernel,
        out_shape=jax.ShapeDtypeStruct((4, columns * UNIT, HEAD_DIM), jnp.bfloat16),
        compiler_params=pltpu.CompilerParams(vmem_limit_bytes=16 * 1024 * 1024),
        cost_estimate=pl.CostEstimate(
            flops=units * 256 * 1024 * 512 * 2, bytes_accessed=2 * 1024 * 1024, transcendentals=0
        ),
        name=name,
    )(*operands)


def shifted(value, shift, sign):
    count = lax.axis_size("grp")

    def along(steps):
        pairs = [(source, (source + steps) % count) for source in range(count)]
        return lambda given: lax.ppermute(given, "grp", pairs)

    branches = [along(sign * steps) for steps in range(1, count)]
    return lax.switch(shift - 1, branches, value)


def exchanged(value):
    return lax.all_to_all(value, "head", split_axis=0, concat_axis=0, tiled=True)


def body(q_nope, q_rope, w_absorb_k, w_absorb_v, latent_cache, new_latent, lengths, moves):
    steps, slots, heads, _ = q_nope.shape
    holders, capacity, entries = latent_cache.shape
    columns = lax.axis_size("head")
    shift = moves[0, 0]
    first_slot = (lax.axis_index("grp") * columns + lax.axis_index("head")) * holders
    counts = lax.dynamic_slice_in_dim(lengths, first_slot, holders)

    q_nope = q_nope.reshape(steps, slots * heads, HEAD_DIM)
    q_rope = q_rope.reshape(steps, slots * heads, ROPE)
    cache = jnp.swapaxes(latent_cache, 1, 2)
    recent = jnp.swapaxes(new_latent, 0, 1)
    moved_out = absorb(q_nope, q_rope, w_absorb_k, columns, (2, 3), [(2, 0)], "absorb_moved")
    held_out = absorb(
        q_nope, q_rope, w_absorb_k, columns, (0, 1, 2, 3), [(0, 0), (0, 1), (2, 1)], "absorb_held"
    )
    moved_in = exchanged(moved_out)
    keys, fresh = prepare(counts, cache, recent)
    moved_in = jnp.concatenate([moved_in, fresh], axis=0)
    held_out, keys, moved_in = lax.optimization_barrier((held_out, keys, moved_in))
    held_in = exchanged(held_out)
    moved_in = shifted(moved_in, shift, -1)
    moved_mixed = attend(
        attend_moved_kernel, counts, moved_in, keys, columns, 1, "attend_moved"
    )
    keys, moved_mixed = lax.optimization_barrier((keys, moved_mixed))
    held_mixed = attend(
        attend_held_kernel, counts, held_in, keys, columns, 3, "attend_held"
    )
    held_mixed, moved_mixed = lax.optimization_barrier((held_mixed, moved_mixed))
    held_back = exchanged(held_mixed)
    moved_back = exchanged(shifted(moved_mixed, shift, 1))
    part = project(project_held_kernel, (held_back, w_absorb_v), 3, "project_held")
    out = project(project_moved_kernel, (moved_back, w_absorb_v, part), 1, "project_moved")
    return out.reshape(steps, slots, heads, HEAD_DIM)


def solution(mesh):
    placed = (
        P(None, "grp", "head", None),
        P(None, "grp", "head", None),
        P("head", None, None),
        P("head", None, None),
        P(("grp", "head"), None, None),
        P(None, ("grp", "head"), None),
        P(),
        P("head", None),
    )
    return jax.shard_map(
        body, mesh=mesh, in_specs=placed, out_specs=P(None, "grp", "head", None), check_vma=False
    )
```

```python
import functools
import math

import jax
import jax.numpy as jnp
from jax import lax
from jax.experimental import pallas as pl
from jax.experimental.pallas import tpu as pltpu
from jax.sharding import PartitionSpec as P

HEAD_DIM = 128
ROPE = 64
LATENT = 512
LANES = 128
CHUNKS = LATENT // LANES
UNIT = 16
MOVED_ROWS = CHUNKS * UNIT + UNIT // 2
PARTS = 4
HIDDEN = -1e30
LOG2_E = 1.4426950408889634

yarn_gain = (0.1 * math.log(40.0) + 1.0) ** 2
score_scale = yarn_gain / math.sqrt(HEAD_DIM + ROPE)


def split_places(rows, columns):
    wide = rows.astype(jnp.float32).reshape(columns, 2, 8, rows.shape[-1])
    return wide[:, 0], wide[:, 1]


def spread_heads(rows, heads):
    columns = rows.shape[0]
    lane_head = lax.broadcasted_iota(jnp.int32, rows.shape, 1) % heads
    pieces = [
        jnp.where(lane_head == head, rows, 0.0)
        .astype(jnp.bfloat16)
        .reshape(columns * UNIT, HEAD_DIM)
        for head in range(heads)
    ]
    return jnp.concatenate(pieces, axis=1)


def absorb_kernel(steps, units, q_hbm, r_hbm, w_hbm, out_ref, q_ref, r_ref, w_ref, sems):
    columns = out_ref.shape[0]
    heads = w_ref.shape[0]
    first = steps[0]
    copies = [
        pltpu.make_async_copy(q_hbm.at[pl.ds(first, len(steps))], q_ref, sems.at[0]),
        pltpu.make_async_copy(r_hbm.at[pl.ds(first, len(steps))], r_ref, sems.at[1]),
    ]
    step = heads // PARTS
    for part in range(PARTS):
        piece = pl.ds(part * step, step)
        copies.append(
            pltpu.make_async_copy(w_hbm.at[piece], w_ref.at[piece], sems.at[2 + part])
        )
    for copy in copies:
        copy.start()
    copies[0].wait()
    nope = {step: split_places(q_ref[step - first], columns) for step in steps}
    copies[1].wait()
    rope = {step: split_places(r_ref[step - first], columns) for step in steps}

    def unit_of(parts, begin, place):
        return jnp.concatenate([parts[begin][place], parts[begin + 1][place]], axis=1)

    at = len(units) * CHUNKS * UNIT
    if len(units) > 1:
        pair = [unit_of(rope, *unit) for unit in units[:2]]
        both = jnp.concatenate(pair, axis=2).astype(jnp.bfloat16)
        out_ref[:, pl.ds(at, UNIT), :] = both
        at += UNIT
    begin, place = units[-1]
    both = jnp.concatenate([rope[begin][place], rope[begin + 1][place]], axis=2)
    out_ref[:, pl.ds(at, UNIT // 2), :] = both.astype(jnp.bfloat16)
    spreads = [spread_heads(unit_of(nope, *unit), heads) for unit in units]
    spread = jnp.concatenate(spreads, axis=0)
    latent = None
    step = heads // PARTS
    for part in range(PARTS):
        copies[2 + part].wait()
        weights = w_ref[pl.ds(part * step, step)].reshape(step * HEAD_DIM, LATENT)
        rows = spread[:, part * step * HEAD_DIM : (part + 1) * step * HEAD_DIM]
        term = jnp.dot(rows, weights, preferred_element_type=jnp.float32)
        latent = term if latent is None else latent + term
    latent = latent.astype(jnp.bfloat16)
    for number in range(len(units)):
        rows = latent[number * columns * UNIT : (number + 1) * columns * UNIT]
        put_unit(out_ref, number * CHUNKS * UNIT, rows)


def absorb(q_nope, q_rope, w_absorb_k, columns, steps, units, name):
    high = len(units) * (CHUNKS * UNIT + UNIT // 2)
    hbm = pl.BlockSpec(memory_space=pltpu.HBM)
    slots = q_nope.shape[1]
    return pl.pallas_call(
        functools.partial(absorb_kernel, steps, units),
        out_shape=pltpu.HBM((columns, high, LANES), jnp.bfloat16),
        in_specs=[hbm] * 3,
        scratch_shapes=[
            pltpu.VMEM((len(steps), slots, HEAD_DIM), jnp.bfloat16),
            pltpu.VMEM((len(steps), slots, ROPE), jnp.bfloat16),
            pltpu.VMEM(w_absorb_k.shape, jnp.bfloat16),
            pltpu.SemaphoreType.DMA((2 + PARTS,)),
        ],
        compiler_params=pltpu.CompilerParams(vmem_limit_bytes=32 * 1024 * 1024),
        cost_estimate=pl.CostEstimate(
            flops=len(units) * 256 * 1024 * 512 * 2,
            bytes_accessed=3 * 1024 * 1024,
            transcendentals=0,
        ),
        name=name,
    )(in_hbm(q_nope), in_hbm(q_rope), in_hbm(w_absorb_k))


def scores_of(query, keys):
    return lax.dot_general(
        query, keys, (((1,), (1,)), ((), ())), preferred_element_type=jnp.float32
    )


def attend_unit(query, keys, live, scores=None):
    if scores is None:
        scores = scores_of(query, keys)
    position = lax.broadcasted_iota(jnp.int32, scores.shape, 1)
    scores = jnp.where(position < live, scores, HIDDEN)
    peak = jnp.max(scores, axis=1, keepdims=True)
    spread = jnp.exp2((scores - peak) * (score_scale * LOG2_E))
    total = jnp.sum(spread, axis=1, keepdims=True)
    mixed = jnp.dot(
        spread.astype(jnp.bfloat16), keys[:, :LATENT], preferred_element_type=jnp.float32
    )
    return (mixed * (1.0 / total)).astype(jnp.bfloat16)


def place_recent(keys_ref, recent, count):
    capacity = keys_ref.shape[0]
    start = jnp.minimum(count // UNIT * UNIT, capacity - 2 * UNIT)
    start = pl.multiple_of(start, UNIT)
    window = keys_ref[pl.ds(start, 2 * UNIT), :].astype(jnp.float32)
    row = start + lax.broadcasted_iota(jnp.int32, window.shape, 0)
    for step in range(recent.shape[0]):
        window = jnp.where(row == count + step, recent[step : step + 1], window)
    keys_ref[pl.ds(start, 2 * UNIT), :] = window.astype(jnp.bfloat16)


def unit_rows(got_ref, at):
    columns = got_ref.shape[0]
    return got_ref[:, pl.ds(at, UNIT), :].reshape(columns * UNIT, LANES)


def unit_latent(got_ref, at):
    return [unit_rows(got_ref, at + chunk * UNIT) for chunk in range(CHUNKS)]


def put_unit(out_ref, at, mixed):
    columns = out_ref.shape[0]
    mixed = mixed.reshape(columns, UNIT, LATENT)
    for chunk in range(CHUNKS):
        out_ref[:, pl.ds(at + chunk * UNIT, UNIT), :] = mixed[
            :, :, chunk * LANES : (chunk + 1) * LANES
        ]


def prepare_kernel(counts_ref, cache_ref, recent_ref, keys_ref, fresh_ref):
    for place in range(cache_ref.shape[0]):
        for at in range(0, cache_ref.shape[2], LANES):
            keys_ref[place, pl.ds(at, LANES), :] = cache_ref[place, :, pl.ds(at, LANES)].T
        recent = recent_ref[place].astype(jnp.float32)
        place_recent(keys_ref.at[place], recent, counts_ref[place])
        if place == 0:
            late = jnp.concatenate([recent[2:], jnp.zeros((6, recent.shape[1]))], axis=0)
            rope = jnp.concatenate([late[:, LATENT:], jnp.zeros((8, ROPE))], axis=1)
            pieces = [late[:, at : at + LANES] for at in range(0, LATENT, LANES)] + [rope]
            pieces.append(jnp.zeros((MOVED_ROWS - 8 * len(pieces), LANES)))
            fresh_ref[0] = jnp.concatenate(pieces, axis=0).astype(jnp.bfloat16)


def prepare(counts, cache, recent):
    places, entries, capacity = cache.shape
    vmem = pl.BlockSpec(memory_space=pltpu.VMEM)
    return pl.pallas_call(
        prepare_kernel,
        out_shape=(
            pltpu.VMEM((places, capacity, entries), jnp.bfloat16),
            pltpu.HBM((1, MOVED_ROWS, LANES), jnp.bfloat16),
        ),
        in_specs=[pl.BlockSpec(memory_space=pltpu.SMEM), vmem, vmem],
        out_specs=(vmem, vmem),
        compiler_params=pltpu.CompilerParams(vmem_limit_bytes=24 * 1024 * 1024),
        cost_estimate=pl.CostEstimate(
            flops=1024 * 1024, bytes_accessed=8 * 1024 * 1024, transcendentals=0
        ),
        name="prepare",
    )(counts, cache, recent)


def step_of_row(rows, first_step):
    return first_step + lax.broadcasted_iota(jnp.int32, (rows, 1), 0) % UNIT // 8


def packed_rope(got_ref, at):
    columns = got_ref.shape[0]
    both = got_ref[:, pl.ds(at, UNIT // 2), :].astype(jnp.float32)
    rope = jnp.concatenate([both[:, :, :ROPE], both[:, :, ROPE:]], axis=1)
    return rope.reshape(columns * UNIT, ROPE).astype(jnp.bfloat16)


def attend_held_kernel(counts_ref, got_ref, keys, out_hbm, out_ref, sems):
    span = CHUNKS * UNIT
    pair = unit_rows(got_ref, 3 * span)
    ropes = [pair[:, :ROPE], pair[:, ROPE:], packed_rope(got_ref, 3 * span + UNIT)]
    sends = []
    jobs = []
    for place, units in enumerate([[(0, 0)], [(1, 0), (2, 2)]]):
        queries = []
        lives = []
        for unit, first_step in units:
            latent = unit_latent(got_ref, unit * span)
            queries.append(jnp.concatenate(latent + [ropes[unit]], axis=1))
            rows = queries[-1].shape[0]
            lives.append(counts_ref[place] + step_of_row(rows, first_step) + 1)
        query = jnp.concatenate(queries, axis=0)
        jobs.append((place, units, query, jnp.concatenate(lives, axis=0), scores_of(query, keys[place])))
    for place, units, query, live, scores in jobs:
        mixed = attend_unit(query, keys[place], live, scores)
        for number, (unit, _) in enumerate(units):
            put_unit(out_ref, unit * span, mixed[number * rows : (number + 1) * rows])
            send = pltpu.make_async_copy(
                out_ref.at[:, pl.ds(unit * span, span), :],
                out_hbm.at[:, pl.ds(unit * span, span), :],
                sems.at[unit],
            )
            send.start()
            sends.append(send)
    for send in sends:
        send.wait()


def attend_moved_kernel(counts_ref, got_ref, keys_ref, out_ref, keys):
    columns = out_ref.shape[0]
    rows = got_ref.at[pl.ds(0, columns)]
    query = jnp.concatenate(unit_latent(rows, 0) + [packed_rope(rows, CHUNKS * UNIT)], axis=1)
    fresh = got_ref[columns].astype(jnp.float32)
    pieces = [fresh[8 * chunk : 8 * chunk + 8] for chunk in range(CHUNKS + 1)]
    fresh = jnp.concatenate(pieces[:CHUNKS] + [pieces[CHUNKS][:, :ROPE]], axis=1)
    count = counts_ref[0]
    live = count + step_of_row(query.shape[0], 2) + 1
    place_recent(keys.at[0], fresh[:2], count + 2)
    put_unit(out_ref, 0, attend_unit(query, keys[0], live))


def in_hbm(value):
    return pltpu.with_memory_space_constraint(value, pltpu.HBM)


def attend(kernel, counts, got, keys, columns, units, name):
    vmem = pl.BlockSpec(memory_space=pltpu.VMEM)
    shape = (columns, units * CHUNKS * UNIT, LANES)
    out_shape = pltpu.HBM(shape, jnp.bfloat16)
    if units > 1:
        call = dict(
            out_shape=out_shape,
            out_specs=pl.BlockSpec(memory_space=pltpu.HBM),
            scratch_shapes=[pltpu.VMEM(shape, jnp.bfloat16), pltpu.SemaphoreType.DMA((units,))],
        )
    else:
        call = dict(
            out_shape=(out_shape, pltpu.VMEM(keys.shape, jnp.bfloat16)),
            out_specs=(vmem, vmem),
            input_output_aliases={2: 1},
        )
    return pl.pallas_call(
        kernel,
        in_specs=[pl.BlockSpec(memory_space=pltpu.SMEM), vmem, vmem],
        compiler_params=pltpu.CompilerParams(vmem_limit_bytes=28 * 1024 * 1024),
        cost_estimate=pl.CostEstimate(
            flops=units * 256 * 1024 * 1152 * 2,
            bytes_accessed=units * 2 * 1024 * 1024,
            transcendentals=units * 256 * 1024,
        ),
        name=name,
        **call,
    )(counts, got, keys)


def project_unit(got_ref, at, w_ref):
    columns = got_ref.shape[0]
    heads = w_ref.shape[0]
    latent = jnp.concatenate(unit_latent(got_ref, at), axis=1)
    row_head = lax.broadcasted_iota(jnp.int32, (columns * UNIT, HEAD_DIM), 0) % heads
    result = jnp.zeros((columns * UNIT, HEAD_DIM), jnp.float32)
    for head in range(0, heads, 2):
        pair = jnp.concatenate([w_ref[head], w_ref[head + 1]], axis=1)
        product = jnp.dot(latent, pair, preferred_element_type=jnp.float32)
        result = jnp.where(row_head == head, product[:, :HEAD_DIM], result)
        result = jnp.where(row_head == head + 1, product[:, HEAD_DIM:], result)
    result = result.reshape(columns, 2, 8, HEAD_DIM)
    return result[:, 0], result[:, 1]


def join_places(near, far):
    rows = jnp.concatenate([near, far], axis=1).astype(jnp.bfloat16)
    return rows.reshape(rows.shape[0] * UNIT, HEAD_DIM)


def project_held_kernel(got_ref, w_ref, out_ref):
    span = CHUNKS * UNIT
    near = project_unit(got_ref, 0, w_ref)
    far = project_unit(got_ref, span, w_ref)
    late = project_unit(got_ref, 2 * span, w_ref)
    for step in range(2):
        out_ref[step] = join_places(near[step], far[step])
        out_ref[2 + step] = join_places(jnp.zeros_like(late[step]), late[step])


def project_moved_kernel(got_ref, w_ref, part_ref, out_ref):
    columns = got_ref.shape[0]
    near = project_unit(got_ref, 0, w_ref)
    for step in range(2):
        far = split_places(part_ref[2 + step], columns)[1]
        out_ref[step] = part_ref[step]
        out_ref[2 + step] = join_places(near[step], far)


def project(kernel, operands, units, name):
    columns = operands[0].shape[0]
    return pl.pallas_call(
        kernel,
        out_shape=jax.ShapeDtypeStruct((4, columns * UNIT, HEAD_DIM), jnp.bfloat16),
        compiler_params=pltpu.CompilerParams(vmem_limit_bytes=16 * 1024 * 1024),
        cost_estimate=pl.CostEstimate(
            flops=units * 256 * 1024 * 512 * 2, bytes_accessed=2 * 1024 * 1024, transcendentals=0
        ),
        name=name,
    )(*operands)


def shifted(value, shift, sign):
    count = lax.axis_size("grp")

    def along(steps):
        pairs = [(source, (source + steps) % count) for source in range(count)]
        return lambda given: lax.ppermute(given, "grp", pairs)

    branches = [along(sign * steps) for steps in range(1, count)]
    return lax.switch(shift - 1, branches, value)


def exchanged(value):
    return lax.all_to_all(value, "head", split_axis=0, concat_axis=0, tiled=True)


def body(q_nope, q_rope, w_absorb_k, w_absorb_v, latent_cache, new_latent, lengths, moves):
    steps, slots, heads, _ = q_nope.shape
    holders, capacity, entries = latent_cache.shape
    columns = lax.axis_size("head")
    shift = moves[0, 0]
    first_slot = (lax.axis_index("grp") * columns + lax.axis_index("head")) * holders
    counts = lax.dynamic_slice_in_dim(lengths, first_slot, holders)

    q_nope = q_nope.reshape(steps, slots * heads, HEAD_DIM)
    q_rope = q_rope.reshape(steps, slots * heads, ROPE)
    cache = jnp.swapaxes(latent_cache, 1, 2)
    recent = jnp.swapaxes(new_latent, 0, 1)
    moved_out = absorb(q_nope, q_rope, w_absorb_k, columns, (2, 3), [(2, 0)], "absorb_moved")
    held_out = absorb(
        q_nope, q_rope, w_absorb_k, columns, (0, 1, 2, 3), [(0, 0), (0, 1), (2, 1)], "absorb_held"
    )
    moved_in = exchanged(moved_out)
    keys, fresh = prepare(counts, cache, recent)
    moved_in = jnp.concatenate([moved_in, fresh], axis=0)
    held_out, keys, moved_in = lax.optimization_barrier((held_out, keys, moved_in))
    held_in = exchanged(held_out)
    moved_in = shifted(moved_in, shift, -1)
    held_mixed = attend(
        attend_held_kernel, counts, held_in, keys, columns, 3, "attend_held"
    )
    moved_in, held_mixed = lax.optimization_barrier((moved_in, held_mixed))
    held_back = exchanged(held_mixed)
    moved_mixed, _ = attend(
        attend_moved_kernel, counts, moved_in, keys, columns, 1, "attend_moved"
    )
    moved_back = exchanged(shifted(moved_mixed, shift, 1))
    part = project(project_held_kernel, (held_back, w_absorb_v), 3, "project_held")
    out = project(project_moved_kernel, (moved_back, w_absorb_v, part), 1, "project_moved")
    return out.reshape(steps, slots, heads, HEAD_DIM)


def solution(mesh):
    placed = (
        P(None, "grp", "head", None),
        P(None, "grp", "head", None),
        P("head", None, None),
        P("head", None, None),
        P(("grp", "head"), None, None),
        P(None, ("grp", "head"), None),
        P(),
        P("head", None),
    )
    return jax.shard_map(
        body, mesh=mesh, in_specs=placed, out_specs=P(None, "grp", "head", None), check_vma=False
    )
```
